256 devices in a mesh: group: 16 (over x, y), tensor: 16 (over z, core).
Axes of the slice: x: 4, y: 4, z: 8, core: 2. Of those that a mesh axis runs over, the one named last changes fastest.
Arguments:
- attended: bfloat16 [6144, 6144], P('group', 'tensor'), may hold values from -6 to 6
- out_weight: bfloat16 [6144, 3072], P('tensor'), may hold values from -0.078125 to 0.078125
- feedback_error: float32 [16, 6144, 3072], P('group', 'tensor'), may hold values from -112 to 112
- right_init: float32 [3072, 32], replicated, may hold values from -6 to 6
- cotangent: bfloat16 [6144, 3072], P(('group', 'tensor')), may hold values from -6 to 6
Outputs:
- projected: bfloat16 [6144, 3072], P(('group', 'tensor'))
- input_grad: bfloat16 [6144, 6144], P('group', 'tensor')
- new_error: float32 [16, 6144, 3072], P('group', 'tensor')
- left_factor: float32 [6144, 32], P('tensor')
- right_factor: float32 [3072, 32], replicated
The draws below stay inside these ranges and needn't reach their ends.
All inputs are finite; a program needn't handle non-finite values.
Results may differ from the reference program's by a relative error of at most 0.008.
Values may be sent and summed in bfloat16 or wider, within the bound.
A program may use at most 64 MiB of HBM per device.

```python
import jax
import jax.numpy as jnp
from jax import lax

D = 6144
DW = 3072
RANK = 32
ROWS_DEV = 384
GROUPS = 16
ROWS = 6144


def with_spikes(entries, own_key, source, target, blocks, factor):
    def block_of(axis_at):
        return (jnp.arange(entries.shape[axis_at]) // (entries.shape[axis_at] // blocks)).reshape((-1,) + (1,) * (entries.ndim - 1 - axis_at))

    near = jax.random.permutation(own_key, blocks)[block_of(target)]
    other_side = (block_of(target) + blocks // 2) % blocks
    return jnp.where((block_of(source) == near) | (block_of(source) == other_side), factor * entries, entries)


def shard_levels(stream_key, dims, cuts, least, largest):
    level, own = 1.0, jax.random.fold_in(stream_key, 6)
    for dim, shards_of in cuts:
        heights = jnp.exp(jax.random.uniform(jax.random.fold_in(own, dim), (shards_of,), jnp.float32, least / len(cuts), largest / len(cuts)))
        level = level * jnp.repeat(heights, dims[dim] // shards_of).reshape([-1 if axis == dim else 1 for axis in range(len(dims))])
    return level


def normal_values(rng, shape, width, bound, cuts=(), held_as=jnp.bfloat16):
    level = shard_levels(rng, shape, cuts, -0.22, 0.18) if cuts else 1.0
    array = jax.random.normal(rng, shape, jnp.float32) * width * level
    return jnp.minimum(jnp.maximum(array, -bound), bound).astype(held_as)


def noise_with(rng, extent, deviation, reach, split, heavy, kind=jnp.bfloat16):
    values = deviation * jax.random.normal(rng, extent, jnp.float32)
    if split:
        values = values * shard_levels(rng, extent, split, -0.22, 0.18)
    return jnp.clip(with_spikes(values, jax.random.fold_in(rng, 3), *heavy), -reach, reach).astype(kind)


def setup_inputs(seed: int = 0) -> dict:
    arg_keys = jax.random.split(jax.random.key(seed), 6)
    attended = noise_with(arg_keys[0], (ROWS, D), 1.0, 6.0, ((0, 16), (1, 16)), (1, 0, 16, 2.0))
    out_weight = normal_values(arg_keys[1], (D, DW), D ** -0.5, 0.078125, ((0, 16),))
    feedback_error = normal_values(arg_keys[2], (GROUPS, D, DW), (ROWS_DEV ** 0.5), 112.0, ((0, 16), (1, 16)), jnp.float32)
    right_init = normal_values(arg_keys[3], (DW, RANK), 1.0, 6.0, (), jnp.float32)
    cotangent = normal_values(arg_keys[4], (ROWS, DW), 1.0, 6.0, ((0, 256),))
    return dict(attended=attended, out_weight=out_weight, feedback_error=feedback_error, right_init=right_init, cotangent=cotangent)


def reference(attended, out_weight, feedback_error, right_init, cotangent):
    highest = lax.Precision.HIGHEST
    projected = jnp.dot(attended.astype(jnp.float32), out_weight.astype(jnp.float32), preferred_element_type=jnp.float32).astype(jnp.bfloat16)
    input_grad = jnp.dot(cotangent.astype(jnp.float32), out_weight.T.astype(jnp.float32), preferred_element_type=jnp.float32).astype(jnp.bfloat16)
    act_groups = attended.reshape(GROUPS, ROWS_DEV, D).astype(jnp.float32)
    cot_groups = cotangent.reshape(GROUPS, ROWS_DEV, DW).astype(jnp.float32)
    moment = jnp.einsum('grf,grd->gfd', act_groups, cot_groups, precision=highest) + feedback_error
    raw_left = jnp.mean(jnp.einsum('gfd,dr->gfr', moment, right_init, precision=highest), axis=0)
    gram = jnp.dot(raw_left.T, raw_left, precision=highest)
    lower = jnp.linalg.cholesky(gram)
    left_factor = jax.scipy.linalg.solve_triangular(lower, raw_left.T, lower=True).T
    right_factor = jnp.mean(jnp.einsum('gfd,fr->gdr', moment, left_factor, precision=highest), axis=0)
    new_error = moment - jnp.dot(left_factor, right_factor.T, precision=highest)[None]
    return (projected, input_grad, new_error, left_factor, right_factor)
```

```python
import jax
import jax.numpy as jnp
from jax import lax
from jax.experimental import pallas as pl
from jax.experimental.pallas import tpu as pltpu
from jax.sharding import PartitionSpec as P

F32, BF16 = jnp.float32, jnp.bfloat16
G, T, Z = 16, 16, 8
F, N, R = 384, 3072, 32
OWN = 24
CHIP = 48
H = N // 2
TILES = 12
NT = (((1,), (1,)), ((), ()))
TN = (((0,), (0,)), ((), ()))


def dot(a, b):
    return jnp.dot(a, b, preferred_element_type=F32)


def dot_nt(a, b):
    return lax.dot_general(a, b, NT, preferred_element_type=F32)


def split3(x):
    hi = x.astype(BF16)
    rest = x - hi.astype(F32)
    mid = rest.astype(BF16)
    lo = (rest - mid.astype(F32)).astype(BF16)
    return jnp.concatenate([hi, mid, lo], axis=0)


def fold_rows(x):
    return x[0:R] + x[R : 2 * R] + x[2 * R : 3 * R]


def fold_cols(x):
    return x[:, 0:R] + x[:, R : 2 * R] + x[:, 2 * R : 3 * R]


def comm_kernel(
    a_ref, c_ref, qt_ref, w_hbm, e_hbm,
    cf_ref, proj_ref, pt_ref, qft_ref,
    e_ref, w_ref, ehi_ref, elo_ref, qs_ref, r3_ref, re_ref, rt_ref,
    cq_all, r_send, r_in, r_all, y_send, y_in, g_all,
    st_ref, sa_in, s16_ref, sb_in, sc_all, sd_ref, sfin_ref,
    cx_in, part_ref, px_send, px_in, rsl_out, rsr_out, rsl_in, rsr_in, fin_out, fin_in,
    e_sem, w_sem, send_sem, cq_sem, r1_sem, r2_sem, y_sem, gr_sem, sb_sem, sc_sem, sd_sem,
    sib_send, sib_recv, ag_send, ag_recv, sibag_send, sibag_recv, rs_send, rs_recv,
):
    me_g, me_t = lax.axis_index("group"), lax.axis_index("tensor")
    z, core = me_t // 2, me_t % 2
    other = 1 - core
    sib = {"tensor": 2 * z + other}
    right = {"tensor": 2 * ((z + 1) % Z) + core}
    left = {"tensor": 2 * ((z + Z - 1) % Z) + core}

    def remote(src, dst, ssem, rsem, dev):
        return pltpu.make_async_remote_copy(
            src_ref=src, dst_ref=dst, send_sem=ssem, recv_sem=rsem,
            device_id=dev, device_id_type=pl.DeviceIdType.MESH,
        )

    def each_peer(count, me, body):
        def step(k, carry):
            body(k, (me + k) % count)
            return carry

        lax.fori_loop(1, count, step, 0)

    e_copies = []
    for i in range(4):
        rows = pl.ds(96 * i, 96)
        cp = pltpu.make_async_copy(e_hbm.at[rows], e_ref.at[rows], e_sem.at[i])
        cp.start()
        e_copies.append(cp)
    w_copy = pltpu.make_async_copy(w_hbm, w_ref, w_sem)
    w_copy.start()

    barrier = pltpu.get_barrier_semaphore()
    each_peer(T, me_t, lambda k, p: pl.semaphore_signal(
        barrier, inc=1, device_id={"tensor": p}, device_id_type=pl.DeviceIdType.MESH))
    each_peer(G, me_g, lambda k, p: pl.semaphore_signal(
        barrier, inc=1, device_id={"group": p}, device_id_type=pl.DeviceIdType.MESH))

    qs_ref[...] = split3(qt_ref[...])
    cq = fold_cols(dot_nt(c_ref[...], qs_ref[...]))
    cq_all[me_t] = jnp.concatenate([cq[0:8], cq[8:16], cq[16:24], jnp.zeros((8, 32), F32)], axis=1)
    pl.semaphore_wait(barrier, T + G - 2)

    def cq_copy(k, src_t, dst_t):
        return remote(cq_all.at[src_t], cq_all.at[src_t], send_sem.at[0, k], cq_sem.at[src_t], {"tensor": dst_t})

    each_peer(T, me_t, lambda k, p: cq_copy(k, me_t, p).start())

    cx_copy = remote(c_ref.at[:, pl.ds(pl.multiple_of(other * H, H), H)], cx_in, sib_send.at[0], sib_recv.at[0], sib)
    cx_copy.start()

    for i in range(4):
        rows = pl.ds(96 * i, 96)
        e_copies[i].wait()
        e = e_ref[rows, :]
        hi = e.astype(BF16)
        lo = (e - hi.astype(F32)).astype(BF16)
        ehi_ref[rows, :] = hi
        elo_ref[rows, :] = lo
        re_ref[rows, :] = fold_cols(dot_nt(hi, qs_ref[...]) + dot_nt(lo, qs_ref[...]))

    cx_copy.wait()
    mine = c_ref[:, pl.ds(pl.multiple_of(core * H, H), H)].astype(F32)
    theirs = cx_in[...].astype(F32)
    first = jnp.where(core == 0, mine, theirs)
    second = jnp.where(core == 0, theirs, mine)
    cf_ref[core, z] = jnp.concatenate([first, second], axis=0).astype(BF16)

    def ag_copy(direction, s):
        if direction == 0:
            origin, dev = (z + Z - (s - 1)) % Z, right
        else:
            origin, dev = (z + (s - 1)) % Z, left
        block = cf_ref.at[core, origin]
        if s == 4:
            block = block.at[:, pl.ds(direction * (H // 2), H // 2)]
        return remote(block, block, ag_send.at[direction, s - 1], ag_recv.at[direction, s - 1], dev)

    def sib_copy(d):
        block = cf_ref.at[core, (z + d) % Z]
        return remote(block, block, sibag_send.at[d], sibag_recv.at[d], sib)

    def ag_start(s):
        if s > 1:
            ag_copy(0, s - 1).wait_recv()
            ag_copy(1, s - 1).wait_recv()
        if s < 5:
            ag_copy(0, s).start()
            ag_copy(1, s).start()
        if s == 1:
            sib_copy(0).start()
        elif s < 5:
            sib_copy(Z - (s - 1)).start()
            sib_copy(s - 1).start()
        else:
            sib_copy(4).start()

    ag_start(1)

    each_peer(T, me_t, lambda k, p: cq_copy(k, p, me_t).wait_recv())
    x = cq_all[...]
    x = jnp.stack([x[:, :, 32 * b : 32 * b + 32] for b in range(3)], axis=1).reshape(F, R)
    rt = re_ref[...].T + fold_rows(dot(split3(x.T), a_ref[...]))
    for p in range(TILES):
        i, j = p // 3, p % 3
        r_send[p] = rt[8 * i : 8 * i + 8, 128 * j : 128 * j + 128]

    def r1_copy(k, src_g, dst_g):
        return remote(r_send.at[dst_g], r_in.at[src_g], send_sem.at[1, k], r1_sem.at[src_g], {"group": dst_g})

    def r1_start(k, p):
        @pl.when(p < TILES)
        def _():
            r1_copy(k, me_g, p).start()

    each_peer(G, me_g, r1_start)

    w_copy.wait()
    for i in range(4):
        cols = pl.ds(pl.multiple_of(other * H + i * 384, 384), 384)
        px_send[:, i * 384 : i * 384 + 384] = dot(a_ref[...], w_ref[:, cols]).astype(BF16)
    px_copy = remote(px_send, px_in, sib_send.at[1], sib_recv.at[1], sib)
    px_copy.start()
    for i in range(4):
        cols = pl.ds(pl.multiple_of(core * H + i * 384, 384), 384)
        part_ref[:, :, i * 384 : i * 384 + 384] = dot(a_ref[...], w_ref[:, cols]).reshape(Z, CHIP, 384)

    def r2_copy(k, src_g, dst_g):
        return remote(r_all.at[src_g], r_all.at[src_g], send_sem.at[2, k], r2_sem.at[src_g], {"group": dst_g})

    @pl.when(me_g < TILES)
    def _():
        each_peer(G, me_g, lambda k, p: r1_copy(k, p, me_g).wait_recv())
        r_in[me_g] = r_send[me_g]
        r_all[me_g] = jnp.sum(r_in[...], axis=0) * (1.0 / G)
        each_peer(G, me_g, lambda k, p: r2_copy(k, me_g, p).start())

    def rs_copy(direction, s):
        out, inn, dev = (rsr_out, rsl_in, right) if direction == 0 else (rsl_out, rsr_in, left)
        src, dst = out.at[s - 1], inn.at[s - 1]
        if s == 1:
            cols = pl.ds(direction * (H // 2), H // 2)
            src, dst = src.at[:, cols], dst.at[:, cols]
        return remote(src, dst, rs_send.at[direction, s - 1], rs_recv.at[direction, s - 1], dev)

    def term(d, cols=slice(None)):
        return part_ref[d, :, cols]

    def rs_start(s):
        for direction in (0, 1):
            d = (z + (5 - s)) % Z if direction == 0 else (z + Z - (5 - s)) % Z
            out, inn = (rsr_out, rsl_in) if direction == 0 else (rsl_out, rsr_in)
            if s == 1:
                cols = slice(direction * (H // 2), (direction + 1) * (H // 2))
                out[0, :, cols] = term(d, cols).astype(BF16)
            else:
                rs_copy(direction, s - 1).wait_recv()
                if s == 2:
                    got = slice(direction * (H // 2), (direction + 1) * (H // 2))
                    rest = slice((1 - direction) * (H // 2), (2 - direction) * (H // 2))
                    out[1, :, got] = (term(d, got) + inn[0, :, got].astype(F32)).astype(BF16)
                    out[1, :, rest] = term(d, rest).astype(BF16)
                else:
                    out[s - 1] = (term(d) + inn[s - 2].astype(F32)).astype(BF16)
            rs_copy(direction, s).start()

    px_copy.wait()
    part_ref[...] += px_in[...].astype(F32).reshape(Z, CHIP, H)
    rs_start(1)

    def r2_wait(k, p):
        @pl.when(p < TILES)
        def _():
            r2_copy(k, p, me_g).wait_recv()

    each_peer(G, me_g, r2_wait)
    for p in range(TILES):
        i, j = p // 3, p % 3
        rt_ref[8 * i : 8 * i + 8, 128 * j : 128 * j + 128] = r_all[p]
    r3_ref[...] = split3(rt_ref[...])

    y = fold_cols(dot_nt(a_ref[...], r3_ref[...])).reshape(T, 3, 8, R)
    y_send[...] = jnp.concatenate([y[:, 0], y[:, 1], y[:, 2], jnp.zeros((T, 8, 32), F32)], axis=2)

    def y_copy(k, src_t, dst_t):
        return remote(y_send.at[dst_t], y_in.at[src_t], send_sem.at[3, k], y_sem.at[src_t], {"tensor": dst_t})

    each_peer(T, me_t, lambda k, p: y_copy(k, me_t, p).start())

    gram = dot_nt(r3_ref[...], r3_ref[...])
    gram = fold_rows(fold_cols(gram))
    g_all[me_t] = jnp.concatenate([gram[8 * i : 8 * i + 8] for i in range(4)], axis=1)

    def g_copy(k, src_t, dst_t):
        return remote(g_all.at[src_t], g_all.at[src_t], send_sem.at[4, k], gr_sem.at[src_t], {"tensor": dst_t})

    each_peer(T, me_t, lambda k, p: g_copy(k, me_t, p).start())

    for i in range(6):
        cols = pl.ds(512 * i, 512)
        st_ref[:, cols] = fold_rows(dot(r3_ref[...], ehi_ref[:, cols]) + dot(r3_ref[...], elo_ref[:, cols]))

    ag_start(2)

    each_peer(T, me_t, lambda k, p: y_copy(k, p, me_t).wait_recv())
    y_in[me_t] = y_send[me_t]
    y_own = jnp.sum(y_in[...], axis=0)
    y_own = jnp.concatenate([y_own[:, 32 * b : 32 * b + 32] for b in range(3)], axis=0)
    y3 = split3(y_own.T)
    for i in range(6):
        cols = pl.ds(512 * i, 512)
        st_ref[:, cols] += fold_rows(dot(y3, c_ref[:, cols]))

    sa_copy = remote(st_ref.at[pl.ds(pl.multiple_of(other * 16, 16), 16)], sa_in, sib_send.at[2], sib_recv.at[2], sib)
    sa_copy.start()
    rs_start(2)
    sa_copy.wait()
    s16_ref[...] = st_ref[pl.ds(pl.multiple_of(core * 16, 16), 16), :] + sa_in[...]

    def tile(ref, p, first_row):
        rows = pl.ds(pl.multiple_of(first_row + 8 * (p // 8), 8), 8)
        return ref.at[rows, pl.ds(pl.multiple_of(384 * (p % 8), 384), 384)]

    def sb_copy(k, src_g, dst_g):
        return remote(tile(s16_ref, dst_g, 0), sb_in.at[src_g], send_sem.at[5, k], sb_sem.at[src_g], {"group": dst_g})

    each_peer(G, me_g, lambda k, p: sb_copy(k, me_g, p).start())
    ag_start(3)

    each_peer(T, me_t, lambda k, p: g_copy(k, p, me_t).wait_recv())
    gram = jnp.sum(g_all[...], axis=0)
    gram = jnp.concatenate([gram[:, 32 * i : 32 * i + 32] for i in range(4)], axis=0)
    row = lax.broadcasted_iota(jnp.int32, (R, R), 0)
    col = lax.broadcasted_iota(jnp.int32, (R, R), 1)
    m = jnp.concatenate([gram, (row == col).astype(F32)], axis=1)
    row = lax.broadcasted_iota(jnp.int32, (R, 2 * R), 0)
    for k in range(R):
        scale = lax.rsqrt(m[k : k + 1, k : k + 1])
        pivot_row = m[k : k + 1, :] * scale
        factor = m[:, k : k + 1] * scale
        m = jnp.where(row > k, m - factor * pivot_row, jnp.where(row == k, pivot_row, m))
    inverse = m[:, R : 2 * R]

    each_peer(G, me_g, lambda k, p: sb_copy(k, p, me_g).wait_recv())
    sb_in[me_g] = tile(s16_ref, me_g, 0)[...]
    sc_all[z] = jnp.sum(sb_in[...], axis=0)

    def sc_copy(k, src_z, dst_z):
        return remote(sc_all.at[src_z], sc_all.at[src_z], send_sem.at[6, k], sc_sem.at[src_z], {"tensor": 2 * dst_z + core})

    each_peer(Z, z, lambda k, p: sc_copy(k, z, p).start())
    rs_start(3)
    each_peer(Z, z, lambda k, p: sc_copy(k, p, z).wait_recv())
    sd_ref[...] = jnp.sum(sc_all[...], axis=0)
    tile(sfin_ref, me_g, core * 16)[...] = sd_ref[...]

    def sd_copy(k, src_g, dst_g):
        return remote(sd_ref, tile(sfin_ref, src_g, core * 16), send_sem.at[7, k], sd_sem.at[src_g], {"group": dst_g})

    each_peer(G, me_g, lambda k, p: sd_copy(k, me_g, p).start())
    ag_start(4)
    high = lax.Precision.HIGHEST
    pt_ref[...] = jnp.dot(inverse, rt_ref[...], precision=high, preferred_element_type=F32)
    each_peer(G, me_g, lambda k, p: sd_copy(k, p, me_g).wait_recv())
    half = sfin_ref.at[pl.ds(pl.multiple_of(core * 16, 16), 16)]
    se_copy = remote(half, half, sib_send.at[3], sib_recv.at[3], sib)
    se_copy.start()
    rs_start(4)
    ag_start(5)
    se_copy.wait()
    for i in range(6):
        cols = pl.ds(512 * i, 512)
        qft_ref[:, cols] = jnp.dot(inverse, sfin_ref[:, cols] * (1.0 / G), precision=high, preferred_element_type=F32)

    rs_copy(0, 4).wait_recv()
    rs_copy(1, 4).wait_recv()
    total = term(z) + rsl_in[3].astype(F32) + rsr_in[3].astype(F32)
    fin_out[...] = jnp.where(core == 0, total[OWN:], total[:OWN]).astype(BF16)
    fin_copy = remote(fin_out, fin_in, sib_send.at[4], sib_recv.at[4], sib)
    fin_copy.start()
    proj_ref[:, pl.ds(pl.multiple_of(core * H, H), H)] = jnp.where(core == 0, total[:OWN], total[OWN:]).astype(BF16)
    fin_copy.wait()
    proj_ref[:, pl.ds(pl.multiple_of(other * H, H), H)] = fin_in[...]

    for d in range(Z):
        sib_copy(d).wait()
    for s in range(1, 5):
        for direction in (0, 1):
            ag_copy(direction, s).wait_send()
            rs_copy(direction, s).wait_send()
    each_peer(T, me_t, lambda k, p: cq_copy(k, me_t, p).wait_send())

    def r1_wait(k, p):
        @pl.when(p < TILES)
        def _():
            r1_copy(k, me_g, p).wait_send()

    each_peer(G, me_g, r1_wait)

    @pl.when(me_g < TILES)
    def _():
        each_peer(G, me_g, lambda k, p: r2_copy(k, me_g, p).wait_send())

    each_peer(T, me_t, lambda k, p: y_copy(k, me_t, p).wait_send())
    each_peer(T, me_t, lambda k, p: g_copy(k, me_t, p).wait_send())
    each_peer(G, me_g, lambda k, p: sb_copy(k, me_g, p).wait_send())
    each_peer(Z, z, lambda k, p: sc_copy(k, z, p).wait_send())
    each_peer(G, me_g, lambda k, p: sd_copy(k, me_g, p).wait_send())


def communicate(attended, cotangent, right_init_t, out_weight, feedback):
    vmem, anywhere = pl.BlockSpec(memory_space=pltpu.VMEM), pl.BlockSpec(memory_space=pl.ANY)
    dma, v = pltpu.SemaphoreType.DMA, pltpu.VMEM
    return pl.pallas_call(
        comm_kernel,
        out_shape=(
            jax.ShapeDtypeStruct((2, Z, CHIP, H), BF16),
            jax.ShapeDtypeStruct((OWN, N), BF16),
            jax.ShapeDtypeStruct((R, F), F32),
            jax.ShapeDtypeStruct((R, N), F32),
        ),
        in_specs=[vmem, vmem, vmem, anywhere, anywhere],
        out_specs=[vmem] * 4,
        scratch_shapes=[
            v((F, N), F32), v((F, N), BF16), v((F, N), BF16), v((F, N), BF16), v((3 * R, N), BF16),
            v((3 * R, F), BF16), v((F, R), F32), v((R, F), F32),
            v((T, 8, 128), F32), v((TILES, 8, 128), F32), v((G, 8, 128), F32), v((TILES, 8, 128), F32),
            v((T, 8, 128), F32), v((T, 8, 128), F32), v((T, 8, 128), F32),
            v((R, N), F32), v((16, N), F32), v((16, N), F32), v((G, 8, 384), F32), v((Z, 8, 384), F32),
            v((8, 384), F32), v((R, N), F32),
            v((OWN, H), BF16), v((Z, CHIP, H), F32), v((F, H), BF16), v((F, H), BF16),
            v((4, CHIP, H), BF16), v((4, CHIP, H), BF16), v((4, CHIP, H), BF16), v((4, CHIP, H), BF16),
            v((OWN, H), BF16), v((OWN, H), BF16),
            dma((4,)), dma, dma((8, 16)), dma((T,)), dma((G,)), dma((G,)), dma((T,)), dma((T,)),
            dma((G,)), dma((Z,)), dma((G,)),
            dma((5,)), dma((5,)), dma((2, 4)), dma((2, 4)), dma((Z,)), dma((Z,)), dma((2, 4)), dma((2, 4)),
        ],
        compiler_params=pltpu.CompilerParams(
            collective_id=0, has_side_effects=True, vmem_limit_bytes=48 * 1024 * 1024
        ),
        name="communicate",
    )(attended, cotangent, right_init_t, out_weight, feedback)


COLS = 512


def finish_kernel(a_ref, pt_ref, c_ref, qft_ref, w_ref, e_ref, err_ref, ig_ref, lhs_ref, acc_ref):
    step = pl.program_id(0)

    @pl.when(step == 0)
    def _():
        pt = pt_ref[...]
        hi = pt.astype(BF16)
        lo = (pt - hi.astype(F32)).astype(BF16)
        stacked = jnp.concatenate([a_ref[...], -hi, -hi, -lo], axis=0)
        lhs_ref[...] = stacked.T
        acc_ref[...] = jnp.zeros_like(acc_ref)

    qt = qft_ref[...]
    hi = qt.astype(BF16)
    lo = (qt - hi.astype(F32)).astype(BF16)
    c = c_ref[0]
    err_ref[...] = e_ref[...] + dot(lhs_ref[...], jnp.concatenate([c, hi, lo, hi], axis=0))
    acc_ref[...] += dot_nt(c, w_ref[...])

    @pl.when(step == pl.num_programs(0) - 1)
    def _():
        ig_ref[...] = acc_ref[...].astype(BF16)


def finish(attended, pt, cf, qft, out_weight, feedback):
    per_half = H // COLS
    return pl.pallas_call(
        finish_kernel,
        grid=(N // COLS,),
        out_shape=(jax.ShapeDtypeStruct((F, N), F32), jax.ShapeDtypeStruct((F, F), BF16)),
        in_specs=[
            pl.BlockSpec((F, F), lambda j: (0, 0)),
            pl.BlockSpec((R, F), lambda j: (0, 0)),
            pl.BlockSpec((1, F, COLS), lambda j: (j // per_half, 0, j % per_half)),
            pl.BlockSpec((R, COLS), lambda j: (0, j)),
            pl.BlockSpec((F, COLS), lambda j: (0, j)),
            pl.BlockSpec((F, COLS), lambda j: (0, j)),
        ],
        out_specs=[pl.BlockSpec((F, COLS), lambda j: (0, j)), pl.BlockSpec((F, F), lambda j: (0, 0))],
        scratch_shapes=[pltpu.VMEM((F, F + 3 * R), BF16), pltpu.VMEM((F, F), F32)],
        compiler_params=pltpu.CompilerParams(vmem_limit_bytes=32 * 1024 * 1024),
        name="finish",
    )(attended, pt, cf, qft, out_weight, feedback)


def per_device(attended, out_weight, feedback_error, right_init, cotangent):
    feedback = feedback_error[0]
    cf, projected, pt, qft = communicate(attended, cotangent, right_init.T, out_weight, feedback)
    new_error, input_grad = finish(attended, pt, cf.reshape(2, F, H), qft, out_weight, feedback)
    return (projected, input_grad, new_error[None], pt.T, qft.T)


def solution(mesh):
    in_specs = (
        P("group", "tensor"),
        P("tensor", None),
        P("group", "tensor", None),
        P(),
        P(("group", "tensor"), None),
    )
    out_specs = (
        P(("group", "tensor"), None),
        P("group", "tensor"),
        P("group", "tensor", None),
        P("tensor", None),
        P(),
    )
    return jax.shard_map(
        per_device, mesh=mesh, in_specs=in_specs, out_specs=out_specs, check_vma=False
    )
```

```python
import jax
import jax.numpy as jnp
from jax import lax
from jax.experimental import pallas as pl
from jax.experimental.pallas import tpu as pltpu
from jax.sharding import PartitionSpec as P

F32, BF16 = jnp.float32, jnp.bfloat16
G, T, Z = 16, 16, 8
F, N, R = 384, 3072, 32
OWN = 24
CHIP = 48
H = N // 2
Q = H // 2
TILES = 12
NT = (((1,), (1,)), ((), ()))
TN = (((0,), (0,)), ((), ()))


def dot(a, b):
    return jnp.dot(a, b, preferred_element_type=F32)


def dot_nt(a, b):
    return lax.dot_general(a, b, NT, preferred_element_type=F32)


def split3(x):
    hi = x.astype(BF16)
    rest = x - hi.astype(F32)
    mid = rest.astype(BF16)
    lo = (rest - mid.astype(F32)).astype(BF16)
    return jnp.concatenate([hi, mid, lo], axis=0)


def fold_rows(x):
    return x[0:R] + x[R : 2 * R] + x[2 * R : 3 * R]


def hops(step, size):
    return min(step, size - step)


GROUP_OFFSETS = sorted(
    ((dx, dy) for dx in range(4) for dy in range(4) if dx or dy), key=lambda d: -hops(d[0], 4) - hops(d[1], 4)
)
TENSOR_OFFSETS = sorted(((dz, dc) for dz in range(Z) for dc in range(2) if dz or dc), key=lambda d: -hops(d[0], Z))
Z_OFFSETS = sorted(range(1, Z), key=lambda d: -hops(d, Z))


def fold_cols(x):
    return x[:, 0:R] + x[:, R : 2 * R] + x[:, 2 * R : 3 * R]


def comm_kernel(
    a_hbm, c_hbm, qt_hbm, w_hbm, e_hbm,
    m_ref, ig_ref, proj_ref, pt_ref, p3_ref, inv_ref, sfin_ref,
    a_ref, c_ref, qt_ref, w_ref, e_ref, at_ref, ehi_ref, elo_ref, qs_ref, r3_ref, re_ref, ret_ref, rt_ref,
    cq_all, r_send, r_in, r_all, g_all,
    st_ref, sa_in, s16_ref, sb_in, sc_all, sd_ref, cf_ref,
    cx_in, part_ref, px_send, px_in, rsl_out, rsr_out, rsl_in, rsr_in, fin_out, fin_in,
    load_sem, send_sem, recv_sem,
    sib_send, sib_recv, ag_send, ag_recv, sibag_send, sibag_recv, rs_send, rs_recv,
):
    me_g, me_t = lax.axis_index("group"), lax.axis_index("tensor")
    x, y = me_g // 4, me_g % 4
    z, core = me_t // 2, me_t % 2
    other = 1 - core
    sib = {"tensor": 2 * z + other}
    right = {"tensor": 2 * ((z + 1) % Z) + core}
    left = {"tensor": 2 * ((z + Z - 1) % Z) + core}
    groups = [((x + dx) % 4) * 4 + (y + dy) % 4 for dx, dy in GROUP_OFFSETS]
    tensors = [2 * ((z + dz) % Z) + (core + dc) % 2 for dz, dc in TENSOR_OFFSETS]
    chips = [(z + dz) % Z for dz in Z_OFFSETS]

    def remote(src, dst, ssem, rsem, dev):
        return pltpu.make_async_remote_copy(
            src_ref=src, dst_ref=dst, send_sem=ssem, recv_sem=rsem,
            device_id=dev, device_id_type=pl.DeviceIdType.MESH,
        )

    def send(phase, src, dst, dev):
        remote(src, dst, send_sem.at[phase], recv_sem.at[phase], dev).start()

    def arrived(phase, like):
        remote(like, like, send_sem.at[phase], recv_sem.at[phase], sib).wait_recv()

    def left_here(phase, like):
        remote(like, like, send_sem.at[phase], recv_sem.at[phase], sib).wait_send()

    def half(c):
        return pl.ds(pl.multiple_of(c * H, H), H)

    def rank_rows(c):
        return pl.ds(pl.multiple_of(c * 16, 16), 16)

    def load(i, src, dst):
        cp = pltpu.make_async_copy(src, dst, load_sem.at[i])
        cp.start()
        return cp

    qt_load, c_load = load(0, qt_hbm, qt_ref), load(1, c_hbm, c_ref)
    e_loads = [load(2 + i, e_hbm.at[pl.ds(96 * i, 96)], e_ref.at[pl.ds(96 * i, 96)]) for i in range(4)]
    a_load, w_load = load(6, a_hbm, a_ref), load(7, w_hbm, w_ref)

    barrier = pltpu.get_barrier_semaphore()
    for p in tensors:
        pl.semaphore_signal(barrier, inc=1, device_id={"tensor": p}, device_id_type=pl.DeviceIdType.MESH)
    for p in groups:
        pl.semaphore_signal(barrier, inc=1, device_id={"group": p}, device_id_type=pl.DeviceIdType.MESH)

    qt_load.wait()
    qs_ref[...] = split3(qt_ref[...])
    c_load.wait()
    cq = fold_cols(dot_nt(c_ref[...], qs_ref[...]))
    cq_all[me_t] = jnp.concatenate([cq[0:8], cq[8:16], cq[16:24], jnp.zeros((8, 32), F32)], axis=1)
    pl.semaphore_wait(barrier, T + G - 2)

    cx_copy = remote(c_ref.at[:, half(other)], cx_in, sib_send.at[0], sib_recv.at[0], sib)
    cx_copy.start()
    for p in tensors:
        send(0, cq_all.at[me_t], cq_all.at[me_t], {"tensor": p})

    def ag_copy(direction, s, q):
        origin, dev = ((z + Z - (s - 1)) % Z, right) if direction == 0 else ((z + (s - 1)) % Z, left)
        piece = cf_ref.at[core, origin, :, pl.ds(q * Q, Q)]
        return remote(piece, piece, ag_send.at[direction, s - 1, q], ag_recv.at[direction, s - 1, q], dev)

    def sib_copy(d, q):
        piece = cf_ref.at[core, (z + d) % Z, :, pl.ds(q * Q, Q)]
        return remote(piece, piece, sibag_send.at[d, q], sibag_recv.at[d, q], sib)

    def ag_step(s, q):
        if s == 0:
            ag_copy(0, 1, q).start()
            ag_copy(1, 1, q).start()
            sib_copy(0, q).start()
        elif s < 4:
            for direction in (0, 1):
                ag_copy(direction, s, q).wait_recv()
                if s < 3 or direction == q:
                    ag_copy(direction, s + 1, q).start()
            sib_copy(Z - s, q).start()
            sib_copy(s, q).start()
        else:
            ag_copy(q, 4, q).wait_recv()
            sib_copy(4, q).start()

    cx_copy.wait()
    mine = c_ref[:, half(core)].astype(F32)
    theirs = cx_in[...].astype(F32)
    first = jnp.where(core == 0, mine, theirs)
    second = jnp.where(core == 0, theirs, mine)
    cf_ref[core, z] = jnp.concatenate([first, second], axis=0).astype(BF16)
    ag_step(0, 0)
    ag_step(0, 1)

    for i in range(4):
        rows = pl.ds(96 * i, 96)
        e_loads[i].wait()
        e = e_ref[rows, :]
        hi = e.astype(BF16)
        lo = (e - hi.astype(F32)).astype(BF16)
        ehi_ref[rows, :] = hi
        elo_ref[rows, :] = lo
        re_ref[rows, :] = fold_cols(dot_nt(hi, qs_ref[...]) + dot_nt(lo, qs_ref[...]))
    ret_ref[...] = re_ref[...].T
    a_load.wait()
    at_ref[...] = a_ref[...].T

    w_load.wait()
    for i in range(4):
        cols = pl.ds(pl.multiple_of(other * H + i * 384, 384), 384)
        px_send[:, i * 384 : i * 384 + 384] = dot(a_ref[...], w_ref[:, cols]).astype(BF16)
    px_copy = remote(px_send, px_in, sib_send.at[1], sib_recv.at[1], sib)
    px_copy.start()
    ag_step(1, 0)

    arrived(0, cq_all.at[pl.ds(0, T - 1)])
    v = cq_all[...]
    v = jnp.stack([v[:, :, 32 * b : 32 * b + 32] for b in range(3)], axis=1).reshape(F, R)
    rt = ret_ref[...] + fold_rows(dot(split3(v.T), a_ref[...]))
    for p in range(TILES):
        i, j = p // 3, p % 3
        r_send[p] = rt[8 * i : 8 * i + 8, 128 * j : 128 * j + 128]

    for p in groups:
        @pl.when(p < TILES)
        def _():
            send(1, r_send.at[p], r_in.at[me_g], {"group": p})

    ag_step(1, 1)
    for i in range(4):
        cols = pl.ds(pl.multiple_of(core * H + i * 384, 384), 384)
        part_ref[:, :, i * 384 : i * 384 + 384] = dot(a_ref[...], w_ref[:, cols]).reshape(Z, CHIP, 384)

    def rs_copy(direction, s):
        out, inn, dev = (rsr_out, rsl_in, right) if direction == 0 else (rsl_out, rsr_in, left)
        src, dst = out.at[s - 1], inn.at[s - 1]
        if s == 1:
            cols = pl.ds(direction * Q, Q)
            src, dst = src.at[:, cols], dst.at[:, cols]
        return remote(src, dst, rs_send.at[direction, s - 1], rs_recv.at[direction, s - 1], dev)

    def rs_step(s):
        for direction in (0, 1):
            d = (z + (5 - s)) % Z if direction == 0 else (z + Z - (5 - s)) % Z
            out, inn = (rsr_out, rsl_in) if direction == 0 else (rsl_out, rsr_in)
            got, rest = slice(direction * Q, direction * Q + Q), slice((1 - direction) * Q, (1 - direction) * Q + Q)
            if s == 1:
                out[0, :, got] = part_ref[d, :, got].astype(BF16)
            else:
                rs_copy(direction, s - 1).wait_recv()
                if s == 2:
                    out[1, :, got] = (part_ref[d, :, got] + inn[0, :, got].astype(F32)).astype(BF16)
                    out[1, :, rest] = part_ref[d, :, rest].astype(BF16)
                else:
                    out[s - 1] = (part_ref[d] + inn[s - 2].astype(F32)).astype(BF16)
            rs_copy(direction, s).start()

    px_copy.wait()
    part_ref[...] += px_in[...].astype(F32).reshape(Z, CHIP, H)
    ag_step(2, 0)

    @pl.when(me_g < TILES)
    def _():
        arrived(1, r_in.at[pl.ds(0, G - 1)])
        r_in[me_g] = r_send[me_g]
        r_all[me_g] = jnp.sum(r_in[...], axis=0) * (1.0 / G)
        for p in groups:
            send(2, r_all.at[me_g], r_all.at[me_g], {"group": p})

    ag_step(2, 1)
    rs_step(1)
    ag_step(3, 0)
    ag_step(3, 1)

    @pl.when(me_g < TILES)
    def _():
        arrived(2, r_all.at[pl.ds(0, TILES - 1)])

    @pl.when(me_g >= TILES)
    def _():
        arrived(2, r_all)

    for p in range(TILES):
        i, j = p // 3, p % 3
        rt_ref[8 * i : 8 * i + 8, 128 * j : 128 * j + 128] = r_all[p]
    r3_ref[...] = split3(rt_ref[...])

    y3 = split3(fold_rows(dot(r3_ref[...], at_ref[...])))
    for i in range(6):
        cols = pl.ds(512 * i, 512)
        st_ref[:, cols] = fold_rows(dot(r3_ref[...], ehi_ref[:, cols]) + dot(r3_ref[...], elo_ref[:, cols]))
    gram = fold_rows(fold_cols(dot_nt(r3_ref[...], r3_ref[...])))
    g_all[me_t] = jnp.concatenate([gram[8 * i : 8 * i + 8] for i in range(4)], axis=1)
    for p in tensors:
        send(3, g_all.at[me_t], g_all.at[me_t], {"tensor": p})
    ag_step(4, 0)
    ag_step(4, 1)

    def add_cotangent(c):
        for i in range(3):
            cols = pl.ds(pl.multiple_of(c * H + 512 * i, 512), 512)
            block = cf_ref[c, :, :, 512 * i : 512 * i + 512].reshape(F, 512)
            st_ref[:, cols] += fold_rows(dot(y3, block))

    def sa_copy(n, c):
        return remote(
            st_ref.at[rank_rows(other), half(c)], sa_in.at[:, half(c)], sib_send.at[2 + n], sib_recv.at[2 + n], sib
        )

    add_cotangent(core)
    sa_copy(0, core).start()
    for d in range(Z):
        for q in (0, 1):
            sib_copy(d, q).wait()
    add_cotangent(other)
    sa_copy(1, other).start()
    sa_copy(0, core).wait_send()
    sa_copy(0, other).wait_recv()
    sa_copy(1, other).wait_send()
    sa_copy(1, core).wait_recv()
    s16_ref[...] = st_ref[rank_rows(core), :] + sa_in[...]

    def tile(ref, p, first_row):
        rows = pl.ds(pl.multiple_of(first_row + 8 * (p // 8), 8), 8)
        return ref.at[rows, pl.ds(pl.multiple_of(384 * (p % 8), 384), 384)]

    for p in groups:
        send(4, tile(s16_ref, p, 0), sb_in.at[me_g], {"group": p})
    rs_step(2)

    for c in (0, 1):
        for i in range(3):
            cols = pl.ds(c * H + 512 * i, 512)
            m_ref[:, cols] = e_ref[:, cols] + dot(at_ref[...], cf_ref[c, :, :, 512 * i : 512 * i + 512].reshape(F, 512))

    arrived(4, sb_in.at[pl.ds(0, G - 1)])
    sb_in[me_g] = tile(s16_ref, me_g, 0)[...]
    sc_all[z] = jnp.sum(sb_in[...], axis=0)
    for p in chips:
        send(5, sc_all.at[z], sc_all.at[z], {"tensor": 2 * p + core})
    rs_step(3)

    arrived(3, g_all.at[pl.ds(0, T - 1)])
    gram = jnp.sum(g_all[...], axis=0)
    gram = jnp.concatenate([gram[:, 32 * i : 32 * i + 32] for i in range(4)], axis=0)
    row = lax.broadcasted_iota(jnp.int32, (R, R), 0)
    col = lax.broadcasted_iota(jnp.int32, (R, R), 1)
    both = jnp.concatenate([gram, (row == col).astype(F32)], axis=1)
    row = lax.broadcasted_iota(jnp.int32, (R, 2 * R), 0)
    for k in range(R):
        scale = lax.rsqrt(both[k : k + 1, k : k + 1])
        pivot_row = both[k : k + 1, :] * scale
        factor = both[:, k : k + 1] * scale
        both = jnp.where(row > k, both - factor * pivot_row, jnp.where(row == k, pivot_row, both))
    inv_ref[...] = both[:, R : 2 * R]

    arrived(5, sc_all.at[pl.ds(0, Z - 1)])
    sd_ref[...] = jnp.sum(sc_all[...], axis=0)
    tile(sfin_ref, me_g, core * 16)[...] = sd_ref[...]
    for p in groups:
        send(6, sd_ref, tile(sfin_ref, me_g, core * 16), {"group": p})

    pt = jnp.dot(inv_ref[...], rt_ref[...], precision=lax.Precision.HIGHEST, preferred_element_type=F32)
    pt_ref[...] = pt
    hi = pt.astype(BF16)
    lo = (pt - hi.astype(F32)).astype(BF16)
    p3_ref[...] = -jnp.concatenate([hi, hi, lo], axis=0)
    rs_step(4)
    back = dot_nt(cf_ref[0].reshape(F, H), w_ref[:, :H]) + dot_nt(cf_ref[1].reshape(F, H), w_ref[:, H:])
    ig_ref[...] = back.astype(BF16)

    arrived(6, sb_in.at[pl.ds(0, G - 1)])
    mine = sfin_ref.at[rank_rows(core)]
    se_copy = remote(mine, mine, sib_send.at[4], sib_recv.at[4], sib)
    se_copy.start()

    rs_copy(0, 4).wait_recv()
    rs_copy(1, 4).wait_recv()
    total = part_ref[z] + rsl_in[3].astype(F32) + rsr_in[3].astype(F32)
    fin_out[...] = jnp.where(core == 0, total[OWN:], total[:OWN]).astype(BF16)
    fin_copy = remote(fin_out, fin_in, sib_send.at[5], sib_recv.at[5], sib)
    fin_copy.start()
    proj_ref[:, half(core)] = jnp.where(core == 0, total[:OWN], total[OWN:]).astype(BF16)
    se_copy.wait()
    fin_copy.wait()
    proj_ref[:, half(other)] = fin_in[...]

    for q in (0, 1):
        for s in range(1, 5):
            for direction in (0, 1):
                if s < 4 or direction == q:
                    ag_copy(direction, s, q).wait_send()
    for s in range(1, 5):
        for direction in (0, 1):
            rs_copy(direction, s).wait_send()
    left_here(0, cq_all.at[pl.ds(0, T - 1)])

    @pl.when(me_g < TILES)
    def _():
        left_here(1, r_in.at[pl.ds(0, TILES - 1)])
        left_here(2, r_in.at[pl.ds(0, G - 1)])

    @pl.when(me_g >= TILES)
    def _():
        left_here(1, r_in.at[pl.ds(0, TILES)])

    left_here(3, g_all.at[pl.ds(0, T - 1)])
    left_here(4, sb_in.at[pl.ds(0, G - 1)])
    left_here(5, sc_all.at[pl.ds(0, Z - 1)])
    left_here(6, sb_in.at[pl.ds(0, G - 1)])


def communicate(attended, cotangent, right_init_t, out_weight, feedback):
    vmem, hbm = pl.BlockSpec(memory_space=pltpu.VMEM), pl.BlockSpec(memory_space=pltpu.HBM)
    dma, v = pltpu.SemaphoreType.DMA, pltpu.VMEM
    return pl.pallas_call(
        comm_kernel,
        out_shape=(
            jax.ShapeDtypeStruct((F, N), F32),
            jax.ShapeDtypeStruct((F, F), BF16),
            jax.ShapeDtypeStruct((OWN, N), BF16),
            jax.ShapeDtypeStruct((R, F), F32),
            jax.ShapeDtypeStruct((3 * R, F), BF16),
            jax.ShapeDtypeStruct((R, R), F32),
            jax.ShapeDtypeStruct((R, N), F32),
        ),
        in_specs=[hbm] * 5,
        out_specs=[vmem] * 7,
        scratch_shapes=[
            v((F, F), BF16), v((OWN, N), BF16), v((R, N), F32), v((F, N), BF16), v((F, N), F32),
            v((F, F), BF16), v((F, N), BF16), v((F, N), BF16), v((3 * R, N), BF16),
            v((3 * R, F), BF16), v((F, R), F32), v((R, F), F32), v((R, F), F32),
            v((T, 8, 128), F32), v((TILES, 8, 128), F32), v((G, 8, 128), F32), v((TILES, 8, 128), F32), v((T, 8, 128), F32),
            v((R, N), F32), v((16, N), F32), v((16, N), F32), v((G, 8, 384), F32), v((Z, 8, 384), F32),
            v((8, 384), F32), v((2, Z, CHIP, H), BF16),
            v((OWN, H), BF16), v((Z, CHIP, H), F32), v((F, H), BF16), v((F, H), BF16),
            v((4, CHIP, H), BF16), v((4, CHIP, H), BF16), v((4, CHIP, H), BF16), v((4, CHIP, H), BF16),
            v((OWN, H), BF16), v((OWN, H), BF16),
            dma((8,)), dma((7,)), dma((7,)),
            dma((6,)), dma((6,)), dma((2, 4, 2)), dma((2, 4, 2)), dma((Z, 2)), dma((Z, 2)), dma((2, 4)), dma((2, 4)),
        ],
        compiler_params=pltpu.CompilerParams(
            collective_id=0, has_side_effects=True, vmem_limit_bytes=40 * 1024 * 1024
        ),
        name="communicate",
    )(attended, cotangent, right_init_t, out_weight, feedback)


COLS = 512


def finish_kernel(
    m_ref, ig_ref, proj_ref, pt_ref, p3_ref, inv_ref, s_ref,
    err_hbm, ig_hbm, proj_hbm, pt_hbm, qt_hbm,
    err_ref, qt_ref, sem, err_sem,
):
    copies = [
        pltpu.make_async_copy(ig_ref, ig_hbm, sem.at[0]),
        pltpu.make_async_copy(proj_ref, proj_hbm, sem.at[1]),
        pltpu.make_async_copy(pt_ref, pt_hbm, sem.at[2]),
    ]
    for cp in copies:
        cp.start()
    p3 = p3_ref[...].T
    for i in range(N // COLS):
        cols = pl.ds(i * COLS, COLS)
        qt = jnp.dot(inv_ref[...], s_ref[:, cols] * (1.0 / G), precision=lax.Precision.HIGHEST, preferred_element_type=F32)
        qt_ref[:, cols] = qt
        hi = qt.astype(BF16)
        lo = (qt - hi.astype(F32)).astype(BF16)
        err_ref[i] = m_ref[:, cols] + dot(p3, jnp.concatenate([hi, lo, hi], axis=0))
        cp = pltpu.make_async_copy(err_ref.at[i], err_hbm.at[:, cols], err_sem.at[i])
        cp.start()
        copies.append(cp)
    cp = pltpu.make_async_copy(qt_ref, qt_hbm, sem.at[3])
    cp.start()
    copies.append(cp)
    for cp in copies:
        cp.wait()


def finish(m, ig, proj, pt, p3, inv, s):
    vmem, hbm = pl.BlockSpec(memory_space=pltpu.VMEM), pl.BlockSpec(memory_space=pltpu.HBM)
    return pl.pallas_call(
        finish_kernel,
        out_shape=(
            jax.ShapeDtypeStruct((F, N), F32),
            jax.ShapeDtypeStruct((F, F), BF16),
            jax.ShapeDtypeStruct((OWN, N), BF16),
            jax.ShapeDtypeStruct((R, F), F32),
            jax.ShapeDtypeStruct((R, N), F32),
        ),
        in_specs=[vmem] * 7,
        out_specs=[hbm] * 5,
        scratch_shapes=[
            pltpu.VMEM((N // COLS, F, COLS), F32), pltpu.VMEM((R, N), F32),
            pltpu.SemaphoreType.DMA((4,)), pltpu.SemaphoreType.DMA((N // COLS,)),
        ],
        compiler_params=pltpu.CompilerParams(vmem_limit_bytes=32 * 1024 * 1024),
        name="finish",
    )(m, ig, proj, pt, p3, inv, s)


def per_device(attended, out_weight, feedback_error, right_init, cotangent):
    operands = (attended, cotangent, right_init.T, out_weight, feedback_error[0])
    parts = communicate(*(pltpu.with_memory_space_constraint(x, pltpu.HBM) for x in operands))
    new_error, input_grad, projected, pt, qt = finish(*parts)
    return (projected, input_grad, new_error[None], pt.T, qt.T)


def solution(mesh):
    in_specs = (
        P("group", "tensor"),
        P("tensor", None),
        P("group", "tensor", None),
        P(),
        P(("group", "tensor"), None),
    )
    out_specs = (
        P(("group", "tensor"), None),
        P("group", "tensor"),
        P("group", "tensor", None),
        P("tensor", None),
        P(),
    )
    return jax.shard_map(
        per_device, mesh=mesh, in_specs=in_specs, out_specs=out_specs, check_vma=False
    )
```

```python
import jax
import jax.numpy as jnp
from jax import lax
from jax.experimental import pallas as pl
from jax.experimental.pallas import tpu as pltpu
from jax.sharding import PartitionSpec as P

F32, BF16 = jnp.float32, jnp.bfloat16
G, T, Z = 16, 16, 8
F, N, R = 384, 3072, 32
OWN = 24
CHIP = 48
H = N // 2
Q = H // 2
PIECES = 4
PIECE = H // PIECES
TILES = 12
NT = (((1,), (1,)), ((), ()))
TN = (((0,), (0,)), ((), ()))


def dot(a, b):
    return jnp.dot(a, b, preferred_element_type=F32)


def dot_nt(a, b):
    return lax.dot_general(a, b, NT, preferred_element_type=F32)


def split3(x):
    hi = x.astype(BF16)
    rest = x - hi.astype(F32)
    mid = rest.astype(BF16)
    lo = (rest - mid.astype(F32)).astype(BF16)
    return jnp.concatenate([hi, mid, lo], axis=0)


def fold_rows(x):
    return x[0:R] + x[R : 2 * R] + x[2 * R : 3 * R]


def hops(step, size):
    return min(step, size - step)


GROUP_OFFSETS = sorted(
    ((dx, dy) for dx in range(4) for dy in range(4) if dx or dy), key=lambda d: -hops(d[0], 4) - hops(d[1], 4)
)
TENSOR_OFFSETS = sorted(((dz, dc) for dz in range(Z) for dc in range(2) if dz or dc), key=lambda d: -hops(d[0], Z))
Z_OFFSETS = sorted(range(1, Z), key=lambda d: -hops(d, Z))


def fold_cols(x):
    return x[:, 0:R] + x[:, R : 2 * R] + x[:, 2 * R : 3 * R]


def comm_kernel(
    a_hbm, c_hbm, qt_hbm, w_hbm, e_hbm,
    m_ref, ig_ref, proj_ref, pt_ref, p3_ref, inv_ref, sfin_ref,
    a_ref, c_ref, qt_ref, w_ref, e_ref, at_ref, ehi_ref, elo_ref, qs_ref, r3_ref, re_ref, ret_ref, rt_ref,
    cq_all, r_send, r_in, r_all, g_all,
    y_ref, y_in, st_ref, sa_in, s16_ref, sb_in, sc_all, sd_ref, cf_ref,
    land, cx_in, part_ref, px_send, px_in, rsl_out, rsr_out, rsl_in, rsr_in, fin_out, fin_in,
    load_sem, send_sem, recv_sem,
    sib_send, sib_recv, land_send, land_recv, ag_send, ag_recv, sibag_send, sibag_recv, rs_send, rs_recv,
):
    me_g, me_t = lax.axis_index("group"), lax.axis_index("tensor")
    x, y = me_g // 4, me_g % 4
    z, core = me_t // 2, me_t % 2
    other = 1 - core
    sib = {"tensor": 2 * z + other}
    right = {"tensor": 2 * ((z + 1) % Z) + core}
    left = {"tensor": 2 * ((z + Z - 1) % Z) + core}
    groups = [((x + dx) % 4) * 4 + (y + dy) % 4 for dx, dy in GROUP_OFFSETS]
    tensors = [2 * ((z + dz) % Z) + (core + dc) % 2 for dz, dc in TENSOR_OFFSETS]
    chips = [(z + dz) % Z for dz in Z_OFFSETS]

    def remote(src, dst, ssem, rsem, dev):
        return pltpu.make_async_remote_copy(
            src_ref=src, dst_ref=dst, send_sem=ssem, recv_sem=rsem,
            device_id=dev, device_id_type=pl.DeviceIdType.MESH,
        )

    def send(phase, src, dst, dev):
        remote(src, dst, send_sem.at[phase], recv_sem.at[phase], dev).start()

    def arrived(phase, like):
        remote(like, like, send_sem.at[phase], recv_sem.at[phase], sib).wait_recv()

    def left_here(phase, like):
        remote(like, like, send_sem.at[phase], recv_sem.at[phase], sib).wait_send()

    def half(c):
        return pl.ds(pl.multiple_of(c * H, H), H)

    def load(i, src, dst):
        cp = pltpu.make_async_copy(src, dst, load_sem.at[i])
        cp.start()
        return cp

    qt_load, c_load = load(0, qt_hbm, qt_ref), load(1, c_hbm, c_ref)
    e_loads = [load(2 + i, e_hbm.at[pl.ds(96 * i, 96)], e_ref.at[pl.ds(96 * i, 96)]) for i in range(4)]
    a_load, w_load = load(6, a_hbm, a_ref), load(7, w_hbm, w_ref)

    barrier = pltpu.get_barrier_semaphore()
    for p in tensors:
        pl.semaphore_signal(barrier, inc=1, device_id={"tensor": p}, device_id_type=pl.DeviceIdType.MESH)
    for p in groups:
        pl.semaphore_signal(barrier, inc=1, device_id={"group": p}, device_id_type=pl.DeviceIdType.MESH)

    qt_load.wait()
    qs_ref[...] = split3(qt_ref[...])
    c_load.wait()
    cq = fold_cols(dot_nt(c_ref[...], qs_ref[...]))
    cq_all[me_t] = jnp.concatenate([cq[0:8], cq[8:16], cq[16:24], jnp.zeros((8, 32), F32)], axis=1)
    pl.semaphore_wait(barrier, T + G - 2)

    for p in tensors:
        send(0, cq_all.at[me_t], cq_all.at[me_t], {"tensor": p})

    def land_copy(direction, h, k):
        to = (z + 1) % Z if direction == 0 else (z + Z - 1) % Z
        return remote(
            c_ref.at[:, pl.ds(h * H + k * PIECE, PIECE)], land.at[direction, core, :, pl.ds(k * PIECE, PIECE)],
            land_send.at[direction, h, k], land_recv.at[direction, core, k], {"tensor": 2 * to + h},
        )

    def land_wait(direction, c, k):
        piece = land.at[direction, c, :, pl.ds(k * PIECE, PIECE)]
        remote(piece, piece, land_send.at[direction, c, k], land_recv.at[direction, c, k], sib).wait_recv()

    def origin(direction, s):
        return (z + Z - s) % Z if direction == 0 else (z + s) % Z

    def ag_copy(direction, s, k):
        piece = cf_ref.at[core, origin(direction, s - 1), :, pl.ds(k * PIECE, PIECE)]
        dev = right if direction == 0 else left
        return remote(piece, piece, ag_send.at[direction, s - 2, k], ag_recv.at[direction, s - 2, k], dev)

    def sib_copy(d, q):
        piece = cf_ref.at[core, (z + d) % Z, :, pl.ds(q * Q, Q)]
        return remote(piece, piece, sibag_send.at[d, q], sibag_recv.at[d, q], sib)

    def goes_round(direction, k):
        return direction == k // (PIECES // 2)

    def ag_step(s, k):
        for direction in (0, 1):
            if s == 1:
                cols = slice(k * PIECE, (k + 1) * PIECE)
                rows = []
                for c in (0, 1):
                    land_wait(direction, c, k)
                    rows.append(land[direction, c, :, cols].astype(F32))
                cf_ref[core, origin(direction, 1), :, cols] = jnp.concatenate(rows, axis=0).astype(BF16)
            elif s < 4 or goes_round(direction, k):
                ag_copy(direction, s, k).wait_recv()
            if s < 3 or (s == 3 and goes_round(direction, k)):
                ag_copy(direction, s + 1, k).start()
        if k % 2 == 1:
            for d in sorted({s, Z - s}):
                sib_copy(d, k // 2).start()

    def land_start(k):
        for direction in (0, 1):
            for h in (0, 1):
                land_copy(direction, h, k).start()

    land_start(0)
    land_start(1)
    cx_copy = remote(c_ref, cx_in, sib_send.at[0], sib_recv.at[0], sib)
    cx_copy.start()

    for i in range(4):
        rows = pl.ds(96 * i, 96)
        e_loads[i].wait()
        e = e_ref[rows, :]
        hi = e.astype(BF16)
        lo = (e - hi.astype(F32)).astype(BF16)
        ehi_ref[rows, :] = hi
        elo_ref[rows, :] = lo
        re_ref[rows, :] = fold_cols(dot_nt(hi, qs_ref[...]) + dot_nt(lo, qs_ref[...]))
        if i > 1:
            land_start(i)
    ret_ref[...] = re_ref[...].T
    a_load.wait()
    at_ref[...] = a_ref[...].T

    w_load.wait()
    for i in range(4):
        cols = pl.ds(pl.multiple_of(other * H + i * 384, 384), 384)
        px_send[:, i * 384 : i * 384 + 384] = dot(a_ref[...], w_ref[:, cols]).astype(BF16)
    px_copy = remote(px_send, px_in, sib_send.at[1], sib_recv.at[1], sib)
    px_copy.start()
    ag_step(1, 0)

    arrived(0, cq_all.at[pl.ds(0, T - 1)])
    v = cq_all[...]
    v = jnp.stack([v[:, :, 32 * b : 32 * b + 32] for b in range(3)], axis=1).reshape(F, R)
    rt = ret_ref[...] + fold_rows(dot(split3(v.T), a_ref[...]))
    for p in range(TILES):
        i, j = p // 3, p % 3
        r_send[p] = rt[8 * i : 8 * i + 8, 128 * j : 128 * j + 128]

    for p in groups:
        @pl.when(p < TILES)
        def _():
            send(1, r_send.at[p], r_in.at[me_g], {"group": p})

    ag_step(1, 1)
    ag_step(1, 2)
    ag_step(1, 3)
    cx_copy.wait()
    mine, theirs = c_ref[...].astype(F32), cx_in[...].astype(F32)
    block = jnp.concatenate([jnp.where(core == 0, mine, theirs), jnp.where(core == 0, theirs, mine)], axis=0)
    for c in (0, 1):
        cf_ref[c, z] = block[:, c * H : (c + 1) * H].astype(BF16)
    for i in range(4):
        cols = pl.ds(pl.multiple_of(core * H + i * 384, 384), 384)
        part_ref[:, :, i * 384 : i * 384 + 384] = dot(a_ref[...], w_ref[:, cols]).reshape(Z, CHIP, 384)

    def rs_copy(direction, s, q):
        out, inn, dev = (rsr_out, rsl_in, right) if direction == 0 else (rsl_out, rsr_in, left)
        cols = pl.ds(q * Q, Q)
        return remote(
            out.at[s - 1, :, cols], inn.at[s - 1, :, cols], rs_send.at[direction, s - 1, q], rs_recv.at[direction, s - 1, q], dev
        )

    def rs_step(s, same):
        for direction in (0, 1):
            q = direction if same else 1 - direction
            d = (z + (5 - s)) % Z if direction == 0 else (z + Z - (5 - s)) % Z
            out, inn = (rsr_out, rsl_in) if direction == 0 else (rsl_out, rsr_in)
            cols = slice(q * Q, q * Q + Q)
            if s == (1 if same else 2):
                out[s - 1, :, cols] = part_ref[d, :, cols].astype(BF16)
            else:
                rs_copy(direction, s - 1, q).wait_recv()
                out[s - 1, :, cols] = (part_ref[d, :, cols] + inn[s - 2, :, cols].astype(F32)).astype(BF16)
            rs_copy(direction, s, q).start()

    ag_step(2, 0)
    ag_step(2, 1)

    @pl.when(me_g < TILES)
    def _():
        arrived(1, r_in.at[pl.ds(0, G - 1)])
        r_in[me_g] = r_send[me_g]
        r_all[me_g] = jnp.sum(r_in[...], axis=0) * (1.0 / G)
        for p in groups:
            send(2, r_all.at[me_g], r_all.at[me_g], {"group": p})

    ag_step(2, 2)
    ag_step(2, 3)
    px_copy.wait_recv()
    part_ref[...] += px_in[...].astype(F32).reshape(Z, CHIP, H)
    for k in range(PIECES):
        ag_step(3, k)
    rs_step(1, True)
    rs_step(2, False)

    @pl.when(me_g < TILES)
    def _():
        arrived(2, r_all.at[pl.ds(0, TILES - 1)])

    @pl.when(me_g >= TILES)
    def _():
        arrived(2, r_all)

    for p in range(TILES):
        i, j = p // 3, p % 3
        rt_ref[8 * i : 8 * i + 8, 128 * j : 128 * j + 128] = r_all[p]
    r3_ref[...] = split3(rt_ref[...])

    y_ref[...] = fold_rows(dot(r3_ref[...], at_ref[...]))
    y_copy = remote(y_ref, y_in, sib_send.at[2], sib_recv.at[2], sib)
    y_copy.start()

    def feedback_term(c):
        for i in range(3):
            cols = pl.ds(pl.multiple_of(c * H + 512 * i, 512), 512)
            st_ref[:, cols] = fold_rows(dot(r3_ref[...], ehi_ref[:, cols]) + dot(r3_ref[...], elo_ref[:, cols]))

    feedback_term(other)
    sa_copy = remote(st_ref.at[:, half(other)], sa_in, sib_send.at[3], sib_recv.at[3], sib)
    sa_copy.start()
    feedback_term(core)
    for k in range(PIECES):
        ag_step(4, k)
    y_copy.wait_recv()
    y3 = split3(y_ref[...] + y_in[...])
    sa_copy.wait_recv()
    for i in range(3):
        cols = slice(512 * i, 512 * i + 512)
        part = st_ref[:, pl.ds(pl.multiple_of(core * H + 512 * i, 512), 512)] + sa_in[:, cols]
        s16_ref[:, cols] = part + fold_rows(dot(y3, cf_ref[core, :, :, cols].reshape(F, 512)))

    def tile(ref, p, first_col):
        rows = pl.ds(pl.multiple_of(8 * (p // 4), 8), 8)
        return ref.at[rows, pl.ds(pl.multiple_of(first_col + 384 * (p % 4), 384), 384)]

    for p in groups:
        send(4, tile(s16_ref, p, 0), sb_in.at[me_g], {"group": p})
    gram = fold_rows(fold_cols(dot_nt(r3_ref[...], r3_ref[...])))
    g_all[me_t] = jnp.concatenate([gram[8 * i : 8 * i + 8] for i in range(4)], axis=1)
    for p in tensors:
        send(3, g_all.at[me_t], g_all.at[me_t], {"tensor": p})
    rs_step(2, True)
    rs_step(3, False)

    for d in range(1, Z):
        for q in (0, 1):
            sib_copy(d, q).wait_recv()
    for c in (0, 1):
        for i in range(3):
            cols = pl.ds(c * H + 512 * i, 512)
            m_ref[:, cols] = e_ref[:, cols] + dot(at_ref[...], cf_ref[c, :, :, 512 * i : 512 * i + 512].reshape(F, 512))

    arrived(4, sb_in.at[pl.ds(0, G - 1)])
    sb_in[me_g] = tile(s16_ref, me_g, 0)[...]
    sc_all[z] = jnp.sum(sb_in[...], axis=0)
    for p in chips:
        send(5, sc_all.at[z], sc_all.at[z], {"tensor": 2 * p + core})
    rs_step(3, True)
    rs_step(4, False)

    arrived(3, g_all.at[pl.ds(0, T - 1)])
    gram = jnp.sum(g_all[...], axis=0)
    gram = jnp.concatenate([gram[:, 32 * i : 32 * i + 32] for i in range(4)], axis=0)
    row = lax.broadcasted_iota(jnp.int32, (R, R), 0)
    col = lax.broadcasted_iota(jnp.int32, (R, R), 1)
    both = jnp.concatenate([gram, (row == col).astype(F32)], axis=1)
    row = lax.broadcasted_iota(jnp.int32, (R, 2 * R), 0)
    for k in range(R):
        scale = lax.rsqrt(both[k : k + 1, k : k + 1])
        pivot_row = both[k : k + 1, :] * scale
        factor = both[:, k : k + 1] * scale
        both = jnp.where(row > k, both - factor * pivot_row, jnp.where(row == k, pivot_row, both))
    inv_ref[...] = both[:, R : 2 * R]

    arrived(5, sc_all.at[pl.ds(0, Z - 1)])
    sd_ref[...] = jnp.sum(sc_all[...], axis=0)
    tile(sfin_ref, me_g, core * H)[...] = sd_ref[...]
    for p in groups:
        send(6, sd_ref, tile(sfin_ref, me_g, core * H), {"group": p})
    rs_step(4, True)

    pt = jnp.dot(inv_ref[...], rt_ref[...], precision=lax.Precision.HIGHEST, preferred_element_type=F32)
    pt_ref[...] = pt
    hi = pt.astype(BF16)
    lo = (pt - hi.astype(F32)).astype(BF16)
    p3_ref[...] = -jnp.concatenate([hi, hi, lo], axis=0).T
    back = dot_nt(cf_ref[0].reshape(F, H), w_ref[:, :H]) + dot_nt(cf_ref[1].reshape(F, H), w_ref[:, H:])
    ig_ref[...] = back.astype(BF16)

    for k in range(PIECES):
        for direction in (0, 1):
            for h in (0, 1):
                land_copy(direction, h, k).wait_send()
            for s in range(2, 5):
                if s < 4 or goes_round(direction, k):
                    ag_copy(direction, s, k).wait_send()
    for s in range(1, 4):
        for direction in (0, 1):
            for q in (0, 1):
                if s > 1 or q == direction:
                    rs_copy(direction, s, q).wait_send()
    px_copy.wait_send()
    y_copy.wait_send()
    sa_copy.wait_send()
    for d in range(1, Z):
        for q in (0, 1):
            sib_copy(d, q).wait_send()
    left_here(0, cq_all.at[pl.ds(0, T - 1)])

    @pl.when(me_g < TILES)
    def _():
        left_here(1, r_in.at[pl.ds(0, TILES - 1)])
        left_here(2, r_in.at[pl.ds(0, G - 1)])

    @pl.when(me_g >= TILES)
    def _():
        left_here(1, r_in.at[pl.ds(0, TILES)])

    left_here(3, g_all.at[pl.ds(0, T - 1)])
    left_here(4, sb_in.at[pl.ds(0, G - 1)])
    left_here(5, sc_all.at[pl.ds(0, Z - 1)])

    for direction in (0, 1):
        for q in (0, 1):
            rs_copy(direction, 4, q).wait_recv()
    total = part_ref[z] + rsl_in[3].astype(F32) + rsr_in[3].astype(F32)
    fin_out[...] = jnp.where(core == 0, total[OWN:], total[:OWN]).astype(BF16)
    fin_copy = remote(fin_out, fin_in, sib_send.at[5], sib_recv.at[5], sib)
    fin_copy.start()
    proj_ref[:, half(core)] = jnp.where(core == 0, total[:OWN], total[OWN:]).astype(BF16)
    arrived(6, sb_in.at[pl.ds(0, G - 1)])
    mine = sfin_ref.at[:, half(core)]
    se_copy = remote(mine, mine, sib_send.at[4], sib_recv.at[4], sib)
    se_copy.start()

    se_copy.wait()
    fin_copy.wait()
    proj_ref[:, half(other)] = fin_in[...]
    for direction in (0, 1):
        for q in (0, 1):
            rs_copy(direction, 4, q).wait_send()
    left_here(6, sb_in.at[pl.ds(0, G - 1)])


def communicate(attended, cotangent, right_init_t, out_weight, feedback):
    vmem, hbm = pl.BlockSpec(memory_space=pltpu.VMEM), pl.BlockSpec(memory_space=pltpu.HBM)
    dma, v = pltpu.SemaphoreType.DMA, pltpu.VMEM
    return pl.pallas_call(
        comm_kernel,
        out_shape=(
            jax.ShapeDtypeStruct((F, N), F32),
            jax.ShapeDtypeStruct((F, F), BF16),
            jax.ShapeDtypeStruct((OWN, N), BF16),
            jax.ShapeDtypeStruct((R, F), F32),
            jax.ShapeDtypeStruct((F, 3 * R), BF16),
            jax.ShapeDtypeStruct((R, R), F32),
            jax.ShapeDtypeStruct((R, N), F32),
        ),
        in_specs=[hbm] * 5,
        out_specs=[vmem] * 7,
        scratch_shapes=[
            v((F, F), BF16), v((OWN, N), BF16), v((R, N), F32), v((F, N), BF16), v((F, N), F32),
            v((F, F), BF16), v((F, N), BF16), v((F, N), BF16), v((3 * R, N), BF16),
            v((3 * R, F), BF16), v((F, R), F32), v((R, F), F32), v((R, F), F32),
            v((T, 8, 128), F32), v((TILES, 8, 128), F32), v((G, 8, 128), F32), v((TILES, 8, 128), F32), v((T, 8, 128), F32),
            v((R, F), F32), v((R, F), F32), v((R, N), F32), v((R, H), F32), v((R, H), F32), v((G, 8, 384), F32), v((Z, 8, 384), F32),
            v((8, 384), F32), v((2, Z, CHIP, H), BF16),
            v((2, 2, OWN, H), BF16), v((OWN, N), BF16), v((Z, CHIP, H), F32), v((F, H), BF16), v((F, H), BF16),
            v((4, CHIP, H), BF16), v((4, CHIP, H), BF16), v((4, CHIP, H), BF16), v((4, CHIP, H), BF16),
            v((OWN, H), BF16), v((OWN, H), BF16),
            dma((8,)), dma((7,)), dma((7,)),
            dma((6,)), dma((6,)), dma((2, 2, PIECES)), dma((2, 2, PIECES)), dma((2, 3, PIECES)), dma((2, 3, PIECES)), dma((Z, 2)), dma((Z, 2)), dma((2, 4, 2)), dma((2, 4, 2)),
        ],
        compiler_params=pltpu.CompilerParams(
            collective_id=0, has_side_effects=True, vmem_limit_bytes=40 * 1024 * 1024
        ),
        name="communicate",
    )(attended, cotangent, right_init_t, out_weight, feedback)


COLS = 512


def finish_kernel(
    m_ref, ig_ref, proj_ref, pt_ref, p3_ref, inv_ref, s_ref,
    err_hbm, ig_hbm, proj_hbm, pt_hbm, qt_hbm,
    err_ref, qt_ref, sem, err_sem,
):
    copies = [
        pltpu.make_async_copy(ig_ref, ig_hbm, sem.at[0]),
        pltpu.make_async_copy(proj_ref, proj_hbm, sem.at[1]),
        pltpu.make_async_copy(pt_ref, pt_hbm, sem.at[2]),
    ]
    for cp in copies:
        cp.start()
    p3 = p3_ref[...]
    for i in range(N // COLS):
        cols = pl.ds(i * COLS, COLS)
        qt = jnp.dot(inv_ref[...], s_ref[:, cols] * (1.0 / G), precision=lax.Precision.HIGHEST, preferred_element_type=F32)
        qt_ref[:, cols] = qt
        hi = qt.astype(BF16)
        lo = (qt - hi.astype(F32)).astype(BF16)
        err_ref[i] = m_ref[:, cols] + dot(p3, jnp.concatenate([hi, lo, hi], axis=0))
        cp = pltpu.make_async_copy(err_ref.at[i], err_hbm.at[:, cols], err_sem.at[i])
        cp.start()
        copies.append(cp)
    cp = pltpu.make_async_copy(qt_ref, qt_hbm, sem.at[3])
    cp.start()
    copies.append(cp)
    for cp in copies:
        cp.wait()


def finish(m, ig, proj, pt, p3, inv, s):
    vmem, hbm = pl.BlockSpec(memory_space=pltpu.VMEM), pl.BlockSpec(memory_space=pltpu.HBM)
    return pl.pallas_call(
        finish_kernel,
        out_shape=(
            jax.ShapeDtypeStruct((F, N), F32),
            jax.ShapeDtypeStruct((F, F), BF16),
            jax.ShapeDtypeStruct((OWN, N), BF16),
            jax.ShapeDtypeStruct((R, F), F32),
            jax.ShapeDtypeStruct((R, N), F32),
        ),
        in_specs=[vmem] * 7,
        out_specs=[hbm] * 5,
        scratch_shapes=[
            pltpu.VMEM((N // COLS, F, COLS), F32), pltpu.VMEM((R, N), F32),
            pltpu.SemaphoreType.DMA((4,)), pltpu.SemaphoreType.DMA((N // COLS,)),
        ],
        compiler_params=pltpu.CompilerParams(vmem_limit_bytes=32 * 1024 * 1024),
        name="finish",
    )(m, ig, proj, pt, p3, inv, s)


def per_device(attended, out_weight, feedback_error, right_init, cotangent):
    operands = (attended, cotangent, right_init.T, out_weight, feedback_error[0])
    parts = communicate(*(pltpu.with_memory_space_constraint(x, pltpu.HBM) for x in operands))
    new_error, input_grad, projected, pt, qt = finish(*parts)
    return (projected, input_grad, new_error[None], pt.T, qt.T)


def solution(mesh):
    in_specs = (
        P("group", "tensor"),
        P("tensor", None),
        P("group", "tensor", None),
        P(),
        P(("group", "tensor"), None),
    )
    out_specs = (
        P(("group", "tensor"), None),
        P("group", "tensor"),
        P("group", "tensor", None),
        P("tensor", None),
        P(),
    )
    return jax.shard_map(
        per_device, mesh=mesh, in_specs=in_specs, out_specs=out_specs, check_vma=False
    )
```

```python
import jax
import jax.numpy as jnp
from jax import lax
from jax.experimental import pallas as pl
from jax.experimental.pallas import tpu as pltpu
from jax.sharding import PartitionSpec as P

F32, BF16 = jnp.float32, jnp.bfloat16
G, T, Z = 16, 16, 8
F, N, R = 384, 3072, 32
OWN = 24
CHIP = 48
H = N // 2
Q = H // 2
PIECES = 4
PIECE = H // PIECES
TILES = 12
NT = (((1,), (1,)), ((), ()))
TN = (((0,), (0,)), ((), ()))


def dot(a, b):
    return jnp.dot(a, b, preferred_element_type=F32)


def dot_nt(a, b):
    return lax.dot_general(a, b, NT, preferred_element_type=F32)


def split3(x):
    hi = x.astype(BF16)
    rest = x - hi.astype(F32)
    mid = rest.astype(BF16)
    lo = (rest - mid.astype(F32)).astype(BF16)
    return jnp.concatenate([hi, mid, lo], axis=0)


def fold_rows(x):
    return x[0:R] + x[R : 2 * R] + x[2 * R : 3 * R]


def hops(step, size):
    return min(step, size - step)


GROUP_OFFSETS = sorted(
    ((dx, dy) for dx in range(4) for dy in range(4) if dx or dy), key=lambda d: -hops(d[0], 4) - hops(d[1], 4)
)
TENSOR_OFFSETS = sorted(((dz, dc) for dz in range(Z) for dc in range(2) if dz or dc), key=lambda d: -hops(d[0], Z))
Z_OFFSETS = sorted(range(1, Z), key=lambda d: -hops(d, Z))


def fold_cols(x):
    return x[:, 0:R] + x[:, R : 2 * R] + x[:, 2 * R : 3 * R]


def comm_kernel(
    a_hbm, c_hbm, qt_hbm, w_hbm, e_hbm,
    m_ref, ig_ref, proj_ref, pt_ref, p3_ref, inv_ref, sfin_ref,
    a_ref, c_ref, qt_ref, w_ref, e_ref, at_ref, ehi_ref, elo_ref, qs_ref, r3_ref, re_ref, ret_ref, rt_ref,
    cq_all, r_send, r_in, r_all, g_all,
    y_ref, y_in, st_ref, sa_in, s16_ref, sb_in, sc_all, sd_ref, cf_ref,
    land, cx_in, part_ref, px_send, px_in, rsl_out, rsr_out, rsl_in, rsr_in, fin_out, fin_in,
    load_sem, send_sem, recv_sem,
    sib_send, sib_recv, land_send, land_recv, ag_send, ag_recv, sibag_send, sibag_recv, rs_send, rs_recv,
):
    me_g, me_t = lax.axis_index("group"), lax.axis_index("tensor")
    x, y = me_g // 4, me_g % 4
    z, core = me_t // 2, me_t % 2
    other = 1 - core
    sib = {"tensor": 2 * z + other}
    right = {"tensor": 2 * ((z + 1) % Z) + core}
    left = {"tensor": 2 * ((z + Z - 1) % Z) + core}
    groups = [((x + dx) % 4) * 4 + (y + dy) % 4 for dx, dy in GROUP_OFFSETS]
    tensors = [2 * ((z + dz) % Z) + (core + dc) % 2 for dz, dc in TENSOR_OFFSETS]
    chips = [(z + dz) % Z for dz in Z_OFFSETS]

    def remote(src, dst, ssem, rsem, dev):
        return pltpu.make_async_remote_copy(
            src_ref=src, dst_ref=dst, send_sem=ssem, recv_sem=rsem,
            device_id=dev, device_id_type=pl.DeviceIdType.MESH,
        )

    def send(phase, src, dst, dev):
        remote(src, dst, send_sem.at[phase], recv_sem.at[phase], dev).start()

    def arrived(phase, like):
        remote(like, like, send_sem.at[phase], recv_sem.at[phase], sib).wait_recv()

    def left_here(phase, like):
        remote(like, like, send_sem.at[phase], recv_sem.at[phase], sib).wait_send()

    def half(c):
        return pl.ds(pl.multiple_of(c * H, H), H)

    def load(i, src, dst):
        cp = pltpu.make_async_copy(src, dst, load_sem.at[i])
        cp.start()
        return cp

    qt_load, c_load = load(0, qt_hbm, qt_ref), load(1, c_hbm, c_ref)
    e_loads = [load(2 + i, e_hbm.at[pl.ds(96 * i, 96)], e_ref.at[pl.ds(96 * i, 96)]) for i in range(4)]
    a_load, w_load = load(6, a_hbm, a_ref), load(7, w_hbm, w_ref)

    barrier = pltpu.get_barrier_semaphore()
    for p in tensors:
        pl.semaphore_signal(barrier, inc=1, device_id={"tensor": p}, device_id_type=pl.DeviceIdType.MESH)
    for p in groups:
        pl.semaphore_signal(barrier, inc=1, device_id={"group": p}, device_id_type=pl.DeviceIdType.MESH)

    qt_load.wait()
    qs_ref[...] = split3(qt_ref[...])
    c_load.wait()
    cq = fold_cols(dot_nt(c_ref[...], qs_ref[...]))
    cq_all[me_t] = jnp.concatenate([cq[0:8], cq[8:16], cq[16:24], jnp.zeros((8, 32), F32)], axis=1)
    pl.semaphore_wait(barrier, T + G - 2)

    for p in tensors:
        send(0, cq_all.at[me_t], cq_all.at[me_t], {"tensor": p})

    def land_copy(direction, h, k):
        to = (z + 1) % Z if direction == 0 else (z + Z - 1) % Z
        return remote(
            c_ref.at[:, pl.ds(h * H + k * PIECE, PIECE)], land.at[direction, core, :, pl.ds(k * PIECE, PIECE)],
            land_send.at[direction, h, k], land_recv.at[direction, core, k], {"tensor": 2 * to + h},
        )

    def land_wait(direction, c, k):
        piece = land.at[direction, c, :, pl.ds(k * PIECE, PIECE)]
        remote(piece, piece, land_send.at[direction, c, k], land_recv.at[direction, c, k], sib).wait_recv()

    def origin(direction, s):
        return (z + Z - s) % Z if direction == 0 else (z + s) % Z

    def ag_copy(direction, s, k):
        piece = cf_ref.at[core, origin(direction, s - 1), :, pl.ds(k * PIECE, PIECE)]
        dev = right if direction == 0 else left
        return remote(piece, piece, ag_send.at[direction, s - 2, k], ag_recv.at[direction, s - 2, k], dev)

    def sib_copy(d, q):
        piece = cf_ref.at[core, (z + d) % Z, :, pl.ds(q * Q, Q)]
        return remote(piece, piece, sibag_send.at[d, q], sibag_recv.at[d, q], sib)

    def goes_round(direction, k):
        return direction == k // (PIECES // 2)

    def ag_step(s, k):
        for direction in (0, 1):
            if s == 1:
                cols = slice(k * PIECE, (k + 1) * PIECE)
                rows = []
                for c in (0, 1):
                    land_wait(direction, c, k)
                    rows.append(land[direction, c, :, cols].astype(F32))
                cf_ref[core, origin(direction, 1), :, cols] = jnp.concatenate(rows, axis=0).astype(BF16)
            elif s < 4 or goes_round(direction, k):
                ag_copy(direction, s, k).wait_recv()
            if s < 3 or (s == 3 and goes_round(direction, k)):
                ag_copy(direction, s + 1, k).start()
        if k % 2 == 1:
            for d in sorted({s, Z - s}):
                sib_copy(d, k // 2).start()

    def land_start(k):
        for direction in (0, 1):
            for h in (0, 1):
                land_copy(direction, h, k).start()

    land_start(0)
    land_start(1)
    cx_copy = remote(c_ref, cx_in, sib_send.at[0], sib_recv.at[0], sib)
    cx_copy.start()

    for i in range(4):
        rows = pl.ds(96 * i, 96)
        e_loads[i].wait()
        e = e_ref[rows, :]
        hi = e.astype(BF16)
        lo = (e - hi.astype(F32)).astype(BF16)
        ehi_ref[rows, :] = hi
        elo_ref[rows, :] = lo
        re_ref[rows, :] = fold_cols(dot_nt(hi, qs_ref[...]) + dot_nt(lo, qs_ref[...]))
        if i > 1:
            land_start(i)
    ret_ref[...] = re_ref[...].T
    a_load.wait()
    at_ref[...] = a_ref[...].T

    w_load.wait()
    for i in range(4):
        cols = pl.ds(pl.multiple_of(other * H + i * 384, 384), 384)
        px_send[:, i * 384 : i * 384 + 384] = dot(a_ref[...], w_ref[:, cols]).astype(BF16)
    px_copy = remote(px_send, px_in, sib_send.at[1], sib_recv.at[1], sib)
    px_copy.start()
    ag_step(1, 0)

    arrived(0, cq_all.at[pl.ds(0, T - 1)])
    v = cq_all[...]
    v = jnp.stack([v[:, :, 32 * b : 32 * b + 32] for b in range(3)], axis=1).reshape(F, R)
    rt = ret_ref[...] + fold_rows(dot(split3(v.T), a_ref[...]))
    for p in range(TILES):
        i, j = p // 3, p % 3
        r_send[p] = rt[8 * i : 8 * i + 8, 128 * j : 128 * j + 128]

    for p in groups:
        @pl.when(p < TILES)
        def _():
            send(1, r_send.at[p], r_in.at[me_g], {"group": p})

    ag_step(1, 1)
    ag_step(1, 2)
    ag_step(1, 3)
    cx_copy.wait()
    mine, theirs = c_ref[...].astype(F32), cx_in[...].astype(F32)
    block = jnp.concatenate([jnp.where(core == 0, mine, theirs), jnp.where(core == 0, theirs, mine)], axis=0)
    for c in (0, 1):
        cf_ref[c, z] = block[:, c * H : (c + 1) * H].astype(BF16)
    for i in range(4):
        cols = pl.ds(pl.multiple_of(core * H + i * 384, 384), 384)
        part_ref[:, :, i * 384 : i * 384 + 384] = dot(a_ref[...], w_ref[:, cols]).reshape(Z, CHIP, 384)

    def rs_copy(direction, s, q):
        out, inn, dev = (rsr_out, rsl_in, right) if direction == 0 else (rsl_out, rsr_in, left)
        cols = pl.ds(q * Q, Q)
        return remote(
            out.at[s - 1, :, cols], inn.at[s - 1, :, cols], rs_send.at[direction, s - 1, q], rs_recv.at[direction, s - 1, q], dev
        )

    def rs_step(s, same):
        for direction in (0, 1):
            q = direction if same else 1 - direction
            d = (z + (5 - s)) % Z if direction == 0 else (z + Z - (5 - s)) % Z
            out, inn = (rsr_out, rsl_in) if direction == 0 else (rsl_out, rsr_in)
            cols = slice(q * Q, q * Q + Q)
            if s == (1 if same else 2):
                out[s - 1, :, cols] = part_ref[d, :, cols].astype(BF16)
            else:
                rs_copy(direction, s - 1, q).wait_recv()
                out[s - 1, :, cols] = (part_ref[d, :, cols] + inn[s - 2, :, cols].astype(F32)).astype(BF16)
            rs_copy(direction, s, q).start()

    ag_step(2, 0)
    ag_step(2, 1)

    @pl.when(me_g < TILES)
    def _():
        arrived(1, r_in.at[pl.ds(0, G - 1)])
        r_in[me_g] = r_send[me_g]
        r_all[me_g] = jnp.sum(r_in[...], axis=0) * (1.0 / G)
        for p in groups:
            send(2, r_all.at[me_g], r_all.at[me_g], {"group": p})

    ag_step(2, 2)
    ag_step(2, 3)
    px_copy.wait_recv()
    part_ref[...] += px_in[...].astype(F32).reshape(Z, CHIP, H)
    for k in range(PIECES):
        ag_step(3, k)
    rs_step(1, True)
    rs_step(2, False)

    @pl.when(me_g < TILES)
    def _():
        arrived(2, r_all.at[pl.ds(0, TILES - 1)])

    @pl.when(me_g >= TILES)
    def _():
        arrived(2, r_all)

    for p in range(TILES):
        i, j = p // 3, p % 3
        rt_ref[8 * i : 8 * i + 8, 128 * j : 128 * j + 128] = r_all[p]
    r3_ref[...] = split3(rt_ref[...])

    y_ref[...] = fold_rows(dot(r3_ref[...], at_ref[...]))
    y_copy = remote(y_ref, y_in, sib_send.at[2], sib_recv.at[2], sib)
    y_copy.start()

    def feedback_term(c):
        for i in range(3):
            cols = pl.ds(pl.multiple_of(c * H + 512 * i, 512), 512)
            st_ref[:, cols] = fold_rows(dot(r3_ref[...], ehi_ref[:, cols]) + dot(r3_ref[...], elo_ref[:, cols]))

    feedback_term(other)
    sa_copy = remote(st_ref.at[:, half(other)], sa_in, sib_send.at[3], sib_recv.at[3], sib)
    sa_copy.start()
    feedback_term(core)
    for k in range(PIECES):
        ag_step(4, k)
    y_copy.wait_recv()
    y3 = split3(y_ref[...] + y_in[...])
    sa_copy.wait_recv()
    for i in range(3):
        cols = slice(512 * i, 512 * i + 512)
        part = st_ref[:, pl.ds(pl.multiple_of(core * H + 512 * i, 512), 512)] + sa_in[:, cols]
        s16_ref[:, cols] = part + fold_rows(dot(y3, cf_ref[core, :, :, cols].reshape(F, 512)))

    def tile(ref, p, first_col):
        rows = pl.ds(pl.multiple_of(8 * (p // 4), 8), 8)
        return ref.at[rows, pl.ds(pl.multiple_of(first_col + 384 * (p % 4), 384), 384)]

    for p in groups:
        send(4, tile(s16_ref, p, 0), sb_in.at[me_g], {"group": p})
    gram = fold_rows(fold_cols(dot_nt(r3_ref[...], r3_ref[...])))
    g_all[me_t] = jnp.concatenate([gram[8 * i : 8 * i + 8] for i in range(4)], axis=1)
    for p in tensors:
        send(3, g_all.at[me_t], g_all.at[me_t], {"tensor": p})
    rs_step(2, True)
    rs_step(3, False)

    for d in range(1, Z):
        for q in (0, 1):
            sib_copy(d, q).wait_recv()
    for c in (0, 1):
        for i in range(3):
            cols = pl.ds(c * H + 512 * i, 512)
            m_ref[:, cols] = e_ref[:, cols] + dot(at_ref[...], cf_ref[c, :, :, 512 * i : 512 * i + 512].reshape(F, 512))

    arrived(4, sb_in.at[pl.ds(0, G - 1)])
    sb_in[me_g] = tile(s16_ref, me_g, 0)[...]
    sc_all[z] = jnp.sum(sb_in[...], axis=0)
    for p in chips:
        send(5, sc_all.at[z], sc_all.at[z], {"tensor": 2 * p + core})
    rs_step(3, True)
    rs_step(4, False)

    arrived(3, g_all.at[pl.ds(0, T - 1)])
    gram = jnp.sum(g_all[...], axis=0)
    gram = jnp.concatenate([gram[:, 32 * i : 32 * i + 32] for i in range(4)], axis=0)
    row = lax.broadcasted_iota(jnp.int32, (R, R), 0)
    col = lax.broadcasted_iota(jnp.int32, (R, R), 1)
    both = jnp.concatenate([gram, (row == col).astype(F32)], axis=1)
    row = lax.broadcasted_iota(jnp.int32, (R, 2 * R), 0)
    for k in range(R):
        scale = lax.rsqrt(both[k : k + 1, k : k + 1])
        pivot_row = both[k : k + 1, :] * scale
        factor = both[:, k : k + 1] * scale
        both = jnp.where(row > k, both - factor * pivot_row, jnp.where(row == k, pivot_row, both))
    inv_ref[...] = both[:, R : 2 * R]

    arrived(5, sc_all.at[pl.ds(0, Z - 1)])
    sd_ref[...] = jnp.sum(sc_all[...], axis=0)
    tile(sfin_ref, me_g, core * H)[...] = sd_ref[...]
    for p in groups:
        send(6, sd_ref, tile(sfin_ref, me_g, core * H), {"group": p})
    rs_step(4, True)

    pt = jnp.dot(inv_ref[...], rt_ref[...], precision=lax.Precision.HIGHEST, preferred_element_type=F32)
    pt_ref[...] = pt
    vt = jnp.dot(inv_ref[...].T, pt * (1.0 / G), precision=lax.Precision.HIGHEST, preferred_element_type=F32)
    hi = vt.astype(BF16)
    lo = (vt - hi.astype(F32)).astype(BF16)
    p3_ref[...] = -jnp.concatenate([hi, hi, lo], axis=0).T
    back = dot_nt(cf_ref[0].reshape(F, H), w_ref[:, :H]) + dot_nt(cf_ref[1].reshape(F, H), w_ref[:, H:])
    ig_ref[...] = back.astype(BF16)

    for k in range(PIECES):
        for direction in (0, 1):
            for h in (0, 1):
                land_copy(direction, h, k).wait_send()
            for s in range(2, 5):
                if s < 4 or goes_round(direction, k):
                    ag_copy(direction, s, k).wait_send()
    for s in range(1, 4):
        for direction in (0, 1):
            for q in (0, 1):
                if s > 1 or q == direction:
                    rs_copy(direction, s, q).wait_send()
    px_copy.wait_send()
    y_copy.wait_send()
    sa_copy.wait_send()
    for d in range(1, Z):
        for q in (0, 1):
            sib_copy(d, q).wait_send()
    left_here(0, cq_all.at[pl.ds(0, T - 1)])

    @pl.when(me_g < TILES)
    def _():
        left_here(1, r_in.at[pl.ds(0, TILES - 1)])
        left_here(2, r_in.at[pl.ds(0, G - 1)])

    @pl.when(me_g >= TILES)
    def _():
        left_here(1, r_in.at[pl.ds(0, TILES)])

    left_here(3, g_all.at[pl.ds(0, T - 1)])
    left_here(4, sb_in.at[pl.ds(0, G - 1)])
    left_here(5, sc_all.at[pl.ds(0, Z - 1)])

    arrived(6, sb_in.at[pl.ds(0, G - 1)])
    mine = sfin_ref.at[:, half(core)]
    se_copy = remote(mine, mine, sib_send.at[4], sib_recv.at[4], sib)
    se_copy.start()

    for direction in (0, 1):
        for q in (0, 1):
            rs_copy(direction, 4, q).wait_recv()
    total = part_ref[z] + rsl_in[3].astype(F32) + rsr_in[3].astype(F32)
    fin_out[...] = jnp.where(core == 0, total[OWN:], total[:OWN]).astype(BF16)
    fin_copy = remote(fin_out, fin_in, sib_send.at[5], sib_recv.at[5], sib)
    fin_copy.start()
    proj_ref[:, half(core)] = jnp.where(core == 0, total[:OWN], total[OWN:]).astype(BF16)
    se_copy.wait()
    fin_copy.wait()
    proj_ref[:, half(other)] = fin_in[...]
    for direction in (0, 1):
        for q in (0, 1):
            rs_copy(direction, 4, q).wait_send()
    left_here(6, sb_in.at[pl.ds(0, G - 1)])


def communicate(attended, cotangent, right_init_t, out_weight, feedback):
    vmem, hbm = pl.BlockSpec(memory_space=pltpu.VMEM), pl.BlockSpec(memory_space=pltpu.HBM)
    dma, v = pltpu.SemaphoreType.DMA, pltpu.VMEM
    return pl.pallas_call(
        comm_kernel,
        out_shape=(
            jax.ShapeDtypeStruct((F, N), F32),
            jax.ShapeDtypeStruct((F, F), BF16),
            jax.ShapeDtypeStruct((OWN, N), BF16),
            jax.ShapeDtypeStruct((R, F), F32),
            jax.ShapeDtypeStruct((F, 3 * R), BF16),
            jax.ShapeDtypeStruct((R, R), F32),
            jax.ShapeDtypeStruct((R, N), F32),
        ),
        in_specs=[hbm] * 5,
        out_specs=[vmem] * 7,
        scratch_shapes=[
            v((F, F), BF16), v((OWN, N), BF16), v((R, N), F32), v((F, N), BF16), v((F, N), F32),
            v((F, F), BF16), v((F, N), BF16), v((F, N), BF16), v((3 * R, N), BF16),
            v((3 * R, F), BF16), v((F, R), F32), v((R, F), F32), v((R, F), F32),
            v((T, 8, 128), F32), v((TILES, 8, 128), F32), v((G, 8, 128), F32), v((TILES, 8, 128), F32), v((T, 8, 128), F32),
            v((R, F), F32), v((R, F), F32), v((R, N), F32), v((R, H), F32), v((R, H), F32), v((G, 8, 384), F32), v((Z, 8, 384), F32),
            v((8, 384), F32), v((2, Z, CHIP, H), BF16),
            v((2, 2, OWN, H), BF16), v((OWN, N), BF16), v((Z, CHIP, H), F32), v((F, H), BF16), v((F, H), BF16),
            v((4, CHIP, H), BF16), v((4, CHIP, H), BF16), v((4, CHIP, H), BF16), v((4, CHIP, H), BF16),
            v((OWN, H), BF16), v((OWN, H), BF16),
            dma((8,)), dma((7,)), dma((7,)),
            dma((6,)), dma((6,)), dma((2, 2, PIECES)), dma((2, 2, PIECES)), dma((2, 3, PIECES)), dma((2, 3, PIECES)), dma((Z, 2)), dma((Z, 2)), dma((2, 4, 2)), dma((2, 4, 2)),
        ],
        compiler_params=pltpu.CompilerParams(
            collective_id=0, has_side_effects=True, vmem_limit_bytes=40 * 1024 * 1024
        ),
        name="communicate",
    )(attended, cotangent, right_init_t, out_weight, feedback)


CHUNKS = ((0, 256), (256, 768), (768, 1280), (1280, 1792), (1792, 2304), (2304, 2816), (2816, 3072))


def finish_kernel(
    m_ref, ig_ref, proj_ref, pt_ref, p3_ref, inv_ref, s_ref,
    err_hbm, ig_hbm, proj_hbm, pt_hbm, qt_hbm,
    err_ref, qt_ref, sem, err_sem,
):
    copies = [
        pltpu.make_async_copy(ig_ref, ig_hbm, sem.at[0]),
        pltpu.make_async_copy(proj_ref, proj_hbm, sem.at[1]),
        pltpu.make_async_copy(pt_ref, pt_hbm, sem.at[2]),
    ]
    for cp in copies:
        cp.start()
    p3 = p3_ref[...]
    for i, (first, last) in enumerate(CHUNKS):
        cols = pl.ds(first, last - first)
        s = s_ref[:, cols]
        hi = s.astype(BF16)
        lo = (s - hi.astype(F32)).astype(BF16)
        err_ref[:, cols] = m_ref[:, cols] + dot(p3, jnp.concatenate([hi, lo, hi], axis=0))
        cp = pltpu.make_async_copy(err_ref.at[:, cols], err_hbm.at[:, cols], err_sem.at[i])
        cp.start()
        copies.append(cp)
    for first, last in CHUNKS:
        cols = pl.ds(first, last - first)
        qt_ref[:, cols] = jnp.dot(
            inv_ref[...], s_ref[:, cols] * (1.0 / G), precision=lax.Precision.HIGHEST, preferred_element_type=F32
        )
    cp = pltpu.make_async_copy(qt_ref, qt_hbm, sem.at[3])
    cp.start()
    copies.append(cp)
    for cp in copies:
        cp.wait()


def finish(m, ig, proj, pt, p3, inv, s):
    vmem, hbm = pl.BlockSpec(memory_space=pltpu.VMEM), pl.BlockSpec(memory_space=pltpu.HBM)
    return pl.pallas_call(
        finish_kernel,
        out_shape=(
            jax.ShapeDtypeStruct((F, N), F32),
            jax.ShapeDtypeStruct((F, F), BF16),
            jax.ShapeDtypeStruct((OWN, N), BF16),
            jax.ShapeDtypeStruct((R, F), F32),
            jax.ShapeDtypeStruct((R, N), F32),
        ),
        in_specs=[vmem] * 7,
        out_specs=[hbm] * 5,
        scratch_shapes=[
            pltpu.VMEM((F, N), F32), pltpu.VMEM((R, N), F32),
            pltpu.SemaphoreType.DMA((4,)), pltpu.SemaphoreType.DMA((len(CHUNKS),)),
        ],
        compiler_params=pltpu.CompilerParams(vmem_limit_bytes=32 * 1024 * 1024),
        name="finish",
    )(m, ig, proj, pt, p3, inv, s)


def per_device(attended, out_weight, feedback_error, right_init, cotangent):
    operands = (attended, cotangent, right_init.T, out_weight, feedback_error[0])
    parts = communicate(*(pltpu.with_memory_space_constraint(x, pltpu.HBM) for x in operands))
    new_error, input_grad, projected, pt, qt = finish(*parts)
    return (projected, input_grad, new_error[None], pt.T, qt.T)


def solution(mesh):
    in_specs = (
        P("group", "tensor"),
        P("tensor", None),
        P("group", "tensor", None),
        P(),
        P(("group", "tensor"), None),
    )
    out_specs = (
        P(("group", "tensor"), None),
        P("group", "tensor"),
        P("group", "tensor", None),
        P("tensor", None),
        P(),
    )
    return jax.shard_map(
        per_device, mesh=mesh, in_specs=in_specs, out_specs=out_specs, check_vma=False
    )
```
